128 devices in a mesh: ctx: 8 (over x_lo, y), grp: 8 (over z, core), head: 2 (over x_hi).
Axes of the slice: x: 4 (x_hi: 2, x_lo: 2; x = x_hi * 2 + x_lo), y: 4, z: 4, core: 2. Of those that a mesh axis runs over, the one named last changes fastest.
Arguments:
- prefill_query: bfloat16 [8192, 8192], P(('ctx', 'grp'), 'head'), may hold values from -400 to 400
- prefill_kv: bfloat16 [8192, 2048], P(('ctx', 'grp'), 'head'), may hold values from -6 to 6
- page_dest: int32 [256, 1], P(('ctx', 'grp')), may hold values from 0 to 7; in each aligned block of 4 rows (0 to 3, 4 to 7, ...) at most 2 rows name the same one
- cache_pool: bfloat16 [8, 8, 128, 32, 2048], P('ctx', 'grp', None, None, 'head'), may hold values from -6 to 6
- page_table: int32 [256, 32], P('grp', 'ctx'), may hold values from 0 to 127, as said below
- context_len: int32 [256], P('grp'), may hold values from 1 to 1024
- dec_query: bfloat16 [4, 256, 8192], P(None, 'grp', 'head'), may hold values from -400 to 400
- dec_new: bfloat16 [4, 256, 2048], P(None, 'grp', 'head'), may hold values from -6 to 6
Outputs:
- prefill_out: bfloat16 [8192, 8192], P(('ctx', 'grp'), 'head')
- arrivals: bfloat16 [8, 8, 16, 32, 2048], P('grp', 'ctx', None, None, 'head')
- dec_out: bfloat16 [4, 256, 8192], P(None, 'grp', 'head')
The draws below stay inside these ranges and needn't reach their ends.
Inputs may be any that keep to these rules, and one draw needn't show every extreme that they name: `page_dest`: the 4 pages of one index of ctx and grp name one decode group at most 2 times. `page_table`: for each decode group and index c of ctx, the entries of columns c * 4 to (c+1) * 4 - 1 over that group's 32 requests name each of its 128 pool pages once.
All inputs are finite; a program needn't handle non-finite values.
Results may differ from the reference program's by a relative error of at most 0.015.
Values may be sent and summed in bfloat16 or wider, within the bound.
A program may use at most 128 MiB of HBM per device.

```python
import math
import jax
import jax.numpy as jnp
import numpy as np
from jax import lax

QH = 64
KVH = 8
HD = 128
PAGE = 32
STEPS = 4
TOK_DEV = 128
REQ_DEV = 32
MAXP = 4
PLEN = 8192
PPAGES = 4
CAP = 2
SLOTS = 16
MAXLEN = 1024
POOL = 128
REQS = 256
N_CTX = 8
N_GRP = 8


def draw_prefill_query(key, part):
    key = jax.random.fold_in(key, 11)
    base = jnp.clip(jax.random.normal(key, (TOK_DEV * N_CTX * N_GRP, QH * HD), jnp.float32), -5.0, 5.0)
    return base.astype(jnp.bfloat16)


def draw_dec_query(key, part):
    key = jax.random.fold_in(key, 23)
    base = jnp.clip(jax.random.normal(key, (STEPS, REQ_DEV * N_GRP, QH * HD), jnp.float32), -5.0, 5.0)
    return base.astype(jnp.bfloat16)


def draw_page_table(key, part):
    key = jax.random.fold_in(key, 37)
    count = REQ_DEV * MAXP
    numbers = jnp.arange(N_GRP * N_CTX)
    perms = jax.vmap(lambda n: jax.random.permutation(jax.random.fold_in(key, n), count))(numbers)
    perms = perms.reshape(N_GRP, N_CTX, REQ_DEV, MAXP)
    perms = jnp.transpose(perms, (0, 2, 1, 3)).reshape(N_GRP * REQ_DEV, N_CTX * MAXP)
    return perms.astype(jnp.int32)


def draw_context_len(key, part):
    key = jax.random.fold_in(key, 41)
    longest = MAXP * PAGE * N_CTX
    first = jax.random.randint(jax.random.fold_in(key, 1), (N_GRP * REQ_DEV,), 1, longest + 1)
    second = jax.random.randint(jax.random.fold_in(key, 2), (N_GRP * REQ_DEV,), 1, longest + 1)
    lengths = jnp.maximum(1, first * second // longest)
    where_long = jax.random.randint(jax.random.fold_in(key, 3), (), 0, N_GRP * REQ_DEV)
    lengths = lengths.at[where_long].set(longest)
    return lengths.astype(jnp.int32)


def shard_levels(key, shape, pieces, smallest, high):
    factor_of, own = 1.0, jax.random.fold_in(key, 6)
    for axis_at, parts in pieces:
        draws = jnp.exp(jax.random.uniform(jax.random.fold_in(own, axis_at), (parts,), jnp.float32, smallest / len(pieces), high / len(pieces)))
        factor_of = factor_of * jnp.repeat(draws, shape[axis_at] // parts).reshape([-1 if axis == axis_at else 1 for axis in range(len(shape))])
    return factor_of


def assign_block(key, own, number, rows, amount, top, limit, lean):
    sequence = jax.random.permutation(key, amount)
    packed, common = load_shares(amount, rows * top, limit, lean, True), load_shares(amount, rows * top, limit, lean, False)
    places = jnp.arange(amount)

    def named(sizes, rotation):
        used = int((sizes > 0).sum())
        fixed = max(1, used // 4)
        shifted = fixed + (places - fixed + rotation * (used - fixed)) % max(1, amount - fixed)
        return jnp.zeros((amount,), jnp.int32).at[sequence[jnp.where(places < fixed, places, shifted)]].set(jnp.asarray(sizes, jnp.int32))

    sizes = jnp.where(number % 4 == 0, named(packed, number // 4), named(common, number - number // 4 - 1))
    mixed = jax.random.permutation(jax.random.fold_in(own, 3), amount)
    source_of, taker = mixed[0:amount // 2 * 2:2], mixed[1:amount // 2 * 2:2]
    room = jnp.minimum(sizes[source_of] - 1, limit - sizes[taker]) // 2
    room = jnp.where((source_of == sequence[0]) | (taker == sequence[0]) | (sizes[taker] == 0), 0, jnp.maximum(room, 0))
    shifted = jax.random.randint(jax.random.fold_in(own, 4), (amount // 2,), 0, 1 << 20) % (room + 1)
    sizes = sizes.at[source_of].add(-shifted).at[taker].add(shifted)
    members = jnp.searchsorted(jnp.cumsum(sizes), jnp.arange(rows * top), side="right").astype(jnp.int32)
    grid = members.reshape(top, rows).T
    grid = grid[jax.random.permutation(jax.random.fold_in(own, 1), rows)]
    rotation = jax.random.randint(jax.random.fold_in(own, 2), (rows, 1), 0, top)
    return jnp.take_along_axis(grid, (jnp.arange(top)[None, :] + rotation) % top, axis=1)


def load_shares(count, total, bound, skew, full):
    weights = [(1 << 20) // math.isqrt(rank ** skew) + 1 for rank in range(1, count + 1)]
    largest = bound if full else min(bound, max(-(-total // count), total * weights[0] // sum(weights)))
    least = 1 if total - largest >= count - 1 else 0
    counts, rest = [largest] + [least] * (count - 1), total - largest - least * (count - 1)
    while rest > 0:
        free = [i for i in range(1, count) if counts[i] < largest] or [i for i in range(1, count) if counts[i] < bound]
        whole, budget = sum([weights[i] for i in free]), rest
        for i in free:
            addition = min(bound - counts[i], max(1, budget * weights[i] // whole), rest)
            counts[i] = counts[i] + addition
            rest = rest - addition
    return np.array(counts)


def normal_values(stream_key, extent, spread, limit, split=(), held_as=jnp.bfloat16):
    entries = spread * jax.random.normal(stream_key, extent, jnp.float32)
    if split:
        entries = entries * shard_levels(stream_key, extent, split, -0.22, 0.18)
    return jnp.clip(entries, -limit, limit).astype(held_as)


def setup_inputs(seed: int = 0) -> dict:
    streams_of = jax.random.split(jax.random.key(seed), 9)
    prefill_query = draw_prefill_query(jax.random.fold_in(streams_of[8], 71), 0)
    prefill_kv = normal_values(streams_of[1], (PLEN, KVH * 2 * HD), 1.0, 6.0, ((0, 64), (1, 2)))
    page_dest_keys = jax.random.split(jax.random.fold_in(streams_of[2], 1), (N_CTX * N_GRP * PPAGES) // PPAGES)
    page_dest_turns = jax.random.permutation(jax.random.fold_in(streams_of[2], 3), (N_CTX * N_GRP * PPAGES) // PPAGES)
    page_dest = jax.vmap(lambda own, number: assign_block(jax.random.fold_in(streams_of[2], 2), own, number, PPAGES, N_GRP, 1, CAP, 2))(page_dest_keys, page_dest_turns).reshape((N_CTX * N_GRP * PPAGES, 1))
    cache_pool = normal_values(streams_of[3], (N_CTX, N_GRP, POOL, PAGE, KVH * 2 * HD), 1.0, 6.0, ((0, 8), (1, 8), (4, 2)))
    page_table = draw_page_table(jax.random.fold_in(streams_of[8], 71), 0)
    context_len = draw_context_len(jax.random.fold_in(streams_of[8], 71), 0)
    dec_query = draw_dec_query(jax.random.fold_in(streams_of[8], 71), 0)
    dec_new = normal_values(streams_of[7], (STEPS, REQS, KVH * 2 * HD), 1.0, 6.0, ((1, 8), (2, 2)))
    return {"prefill_query": prefill_query, "prefill_kv": prefill_kv, "page_dest": page_dest, "cache_pool": cache_pool, "page_table": page_table, "context_len": context_len, "dec_query": dec_query, "dec_new": dec_new}


NEG = -1.0e30


def prefill_head(items):
    query, keys, values = items
    scale = HD ** -0.5
    group = QH // KVH
    qblock = 512 if PLEN % 512 == 0 else PLEN
    blocks = query.reshape(PLEN // qblock, qblock, group, HD)
    starts = jnp.arange(PLEN // qblock, dtype=jnp.int32) * qblock
    keys_f = keys.astype(jnp.float32)
    values_f = values.astype(jnp.float32)

    def one_block(args):
        part, first = args
        score = jnp.einsum("igd,jd->gij", part.astype(jnp.float32), keys_f) * scale
        allowed = jnp.arange(PLEN, dtype=jnp.int32)[None, :] <= (first + jnp.arange(qblock, dtype=jnp.int32))[:, None]
        masked = jnp.where(allowed[None], score, NEG)
        top = jnp.max(masked, axis=-1)
        expo = jnp.where(allowed[None], jnp.exp(masked - top[..., None]), 0.0)
        total = jnp.sum(expo, axis=-1)
        weight = expo.astype(jnp.bfloat16)
        summed = jnp.einsum("gij,jd->igd", weight.astype(jnp.float32), values_f)
        return (summed / jnp.transpose(total)[:, :, None]).astype(jnp.bfloat16)

    outs = lax.map(one_block, (blocks, starts))
    return outs.reshape(PLEN, group, HD)


def decode_group(items):
    query, fresh, pool, table, lengths = items
    scale = HD ** -0.5
    group = QH // KVH
    tab = table.reshape(REQ_DEV, N_CTX, MAXP)
    shard_ids = jnp.arange(N_CTX)[None, :, None]
    cached = pool[shard_ids, tab]
    cached = cached.reshape(REQ_DEV, MAXLEN, KVH, 2, HD).astype(jnp.float32)
    newkv = fresh.reshape(STEPS, REQ_DEV, KVH, 2, HD).astype(jnp.float32)
    quer = query.reshape(STEPS, REQ_DEV, KVH, group, HD).astype(jnp.float32)
    s_old = jnp.einsum("trkgd,rjkd->trkgj", quer, cached[:, :, :, 0]) * scale
    s_new = jnp.einsum("trkgd,urkd->trkgu", quer, newkv[:, :, :, 0]) * scale
    valid = jnp.arange(MAXLEN)[None, :] < lengths[:, None]
    new_ok = jnp.arange(STEPS)[None, :] <= jnp.arange(STEPS)[:, None]
    mask_old = jnp.broadcast_to(valid[None, :, None, None, :], s_old.shape)
    mask_new = jnp.broadcast_to(new_ok[:, None, None, None, :], s_new.shape)
    score = jnp.concatenate([s_old, s_new], axis=-1)
    mask = jnp.concatenate([mask_old, mask_new], axis=-1)
    masked = jnp.where(mask, score, NEG)
    top = jnp.max(masked, axis=-1)
    expo = jnp.where(mask, jnp.exp(masked - top[..., None]), 0.0)
    total = jnp.sum(expo, axis=-1)
    weight = expo.astype(jnp.bfloat16).astype(jnp.float32)
    summed = jnp.einsum("trkgj,rjkd->trkgd", weight[..., :MAXLEN], cached[:, :, :, 1])
    summed = summed + jnp.einsum("trkgu,urkd->trkgd", weight[..., MAXLEN:], newkv[:, :, :, 1])
    result = summed / total[..., None]
    return result.reshape(STEPS, REQ_DEV, QH * HD).astype(jnp.bfloat16)


def reference(prefill_query, prefill_kv, page_dest, cache_pool, page_table, context_len, dec_query, dec_new):
    group = QH // KVH
    query = prefill_query.reshape(PLEN, KVH, group, HD)
    query = jnp.transpose(query, (1, 0, 2, 3))
    pair = prefill_kv.reshape(PLEN, KVH, 2, HD)
    pair = jnp.transpose(pair, (1, 0, 2, 3))
    heads = lax.map(prefill_head, (query, pair[:, :, 0], pair[:, :, 1]))
    prefill_out = jnp.transpose(heads, (1, 0, 2, 3)).reshape(PLEN, QH * HD)

    dest = page_dest.reshape(N_CTX, N_GRP, PPAGES)
    earlier = jnp.arange(PPAGES)[None, :] < jnp.arange(PPAGES)[:, None]
    same = dest[..., :, None] == dest[..., None, :]
    rank = jnp.sum(jnp.logical_and(same, earlier[None, None]), axis=-1)
    target = jnp.arange(N_GRP)[:, None, None, None, None]
    slot_rank = jnp.arange(CAP)[None, None, None, :, None]
    hit = jnp.logical_and(dest[None, :, :, None, :] == target, rank[None, :, :, None, :] == slot_rank)
    index = jnp.sum(jnp.where(hit, jnp.arange(PPAGES)[None, None, None, None, :], 0), axis=-1).astype(jnp.int32)
    found = jnp.any(hit, axis=-1)
    pages = prefill_kv.reshape(N_CTX, N_GRP, PPAGES, PAGE, KVH * 2 * HD)
    shard = jnp.arange(N_CTX)[None, :, None, None]
    source = jnp.arange(N_GRP)[None, None, :, None]
    picked = pages[shard, source, index]
    picked = jnp.where(found[..., None, None], picked, jnp.zeros_like(picked))
    arrivals = picked.reshape(N_GRP, N_CTX, SLOTS, PAGE, KVH * 2 * HD)

    quer = jnp.transpose(dec_query.reshape(STEPS, N_GRP, REQ_DEV, QH * HD), (1, 0, 2, 3))
    fresh = jnp.transpose(dec_new.reshape(STEPS, N_GRP, REQ_DEV, KVH * 2 * HD), (1, 0, 2, 3))
    pool = jnp.transpose(cache_pool, (1, 0, 2, 3, 4))
    table = page_table.reshape(N_GRP, REQ_DEV, N_CTX * MAXP)
    lengths = context_len.reshape(N_GRP, REQ_DEV)
    outs = lax.map(decode_group, (quer, fresh, pool, table, lengths))
    dec_out = jnp.transpose(outs, (1, 0, 2, 3)).reshape(STEPS, REQS, QH * HD)
    return prefill_out, arrivals, dec_out
```

```python
import jax
import jax.numpy as jnp
from jax import lax
from jax.experimental import pallas as pl
from jax.experimental.pallas import tpu as pltpu
from jax.sharding import PartitionSpec as P

HD = 128
NEG = -1e30
SCALE = HD**-0.5
EXP2 = SCALE * 1.4426950408889634
MESH = pl.DeviceIdType.MESH
CHAIN = 256


def softmax_step(s, v, state):
    m, l, acc = state
    mn = jnp.maximum(m, jnp.max(s, axis=1, keepdims=True))
    al = jnp.exp2((m - mn) * EXP2)
    p = jnp.exp2((s - mn) * EXP2)
    part = p[:, 0:HD]
    for t in range(1, s.shape[1] // HD):
        part = part + p[:, t * HD : (t + 1) * HD]
    acc = acc * al + jnp.dot(p.astype(jnp.bfloat16), v, preferred_element_type=jnp.float32)
    return mn, l * al + part, acc


def flash_chunk(qs, k, v, states, allowed):
    def score(q):
        s = lax.dot_general(q, k, (((1,), (1,)), ((), ())), preferred_element_type=jnp.float32)
        return s if allowed is None else jnp.where(allowed, s, NEG)

    out = []
    s = score(qs[0])
    for i in range(len(qs)):
        following = score(qs[i + 1]) if i + 1 < len(qs) else None
        out.append(softmax_step(s, v, states[i]))
        s = following
    return tuple(out)


def kernel(
    pq_ref, pkv_ref, dest_ref, pool_ref, table_ref, len_ref, dq_ref, dn_ref,
    out_ref, arr_ref, dec_ref,
    kv, qin, obuf, pages, arr_send, pool, dq, dn, qd, dec_send, stat_send, dec_recv, stat_recv, fin, finb,
    local_sem, q_send, q_recv, kv_send, kv_recv, o_send, o_recv, a_send, a_recv,
    d_send, d_recv, s_send, s_recv, f_send, f_recv,
):
    c, g = lax.axis_index("ctx"), lax.axis_index("grp")
    x, y, z, co = c // 4, c % 4, g // 2, g % 2
    py = y // 2
    hy = (y % 2 + py) % 2
    k = x * 2 + hy
    ox = 1 - x
    yx = y + 1 - 2 * (y % 2)
    my = 3 - y
    myx = my + 1 - 2 * (my % 2)
    gm = z * 2 + 1 - co

    c_a, c_b, c_c = x * 4 + yx, ox * 4 + my, ox * 4 + myx
    q_peers = [
        (c_a, g, x * 2 + 1 - hy),
        (c_b, gm, ox * 2 + hy),
        (c_c, gm, ox * 2 + 1 - hy),
    ]
    kv_peers = [
        (c_a, g, x * 2 + 1 - hy),
        (ox * 4 + y, g, ox * 2 + hy),
        (ox * 4 + yx, g, ox * 2 + 1 - hy),
    ]

    def dev(cc, gg):
        return {"ctx": cc, "grp": gg}

    def remote(src, dst, send, recv, cc, gg):
        return pltpu.make_async_remote_copy(
            src_ref=src, dst_ref=dst, send_sem=send, recv_sem=recv, device_id=dev(cc, gg), device_id_type=MESH
        )

    loads = [
        pltpu.make_async_copy(dq_ref, dq, local_sem.at[0]),
        pltpu.make_async_copy(dn_ref, dn, local_sem.at[1]),
        pltpu.make_async_copy(pkv_ref, pages, local_sem.at[2]),
        pltpu.make_async_copy(pool_ref, pool, local_sem.at[3]),
    ]
    own_q = pltpu.make_async_copy(pq_ref.at[:, pl.ds(pl.multiple_of(k * 1024, 1024), 1024)], qin.at[3], local_sem.at[4])
    own_kv = pltpu.make_async_copy(pkv_ref.at[:, pl.ds(pl.multiple_of(k * 256, 256), 256)], kv.at[x, y, g], local_sem.at[5])
    own_kv.start()
    own_q.start()
    for load in loads:
        load.start()

    barrier = pltpu.get_barrier_semaphore()
    partners = [((c + i) % 8, g) for i in range(1, 8)] + [(c, (g + i) % 8) for i in range(1, 8)]
    partners += [(c_b, gm), (c_c, gm)]
    for cc, gg in partners:
        pl.semaphore_signal(barrier, inc=1, device_id=dev(cc, gg), device_id_type=MESH)
    pl.semaphore_wait(barrier, len(partners))

    kv_first = []
    for i, (cc, gg, kk) in enumerate(kv_peers):
        kv_first.append(
            remote(pkv_ref.at[:, pl.ds(pl.multiple_of(kk * 256, 256), 256)], kv.at[x, y, g], kv_send.at[i], kv_recv.at[i], cc, gg)
        )
        kv_first[-1].start()
    q_copies = []
    for i, (cc, gg, kk) in enumerate(q_peers):
        q_copies.append(
            remote(pq_ref.at[:, pl.ds(pl.multiple_of(kk * 1024, 1024), 1024)], qin.at[i], q_send.at[i], q_recv.at[i], cc, gg)
        )
        q_copies[-1].start()

    own_kv.wait()
    for i, (cc, gg, kk) in enumerate(kv_peers):
        here = kv.at[cc // 4, cc % 4, gg]
        remote(here, here, kv_send.at[i], kv_recv.at[i], cc, gg).wait_recv()

    mine = kv.at[:, pl.ds(2 * py, 2), g]
    theirs = kv.at[:, pl.ds(2 - 2 * py, 2), g]
    y_copy = remote(mine, mine, kv_send.at[3], kv_recv.at[3], x * 4 + my, g)
    y_copy.start()
    z_peers = [((z + d) % 4) * 2 + co for d in (1, 3, 2)]
    z_from = [((z + 4 - d) % 4) * 2 + co for d in (1, 3, 2)]
    z_copies = []
    for i, gg in enumerate(z_peers):
        z_copies.append(remote(mine, mine, kv_send.at[4 + i], kv_recv.at[4 + i], c, gg))
        z_copies[-1].start()
    sib = gm

    loads[0].wait()
    for t in range(4):
        for head in range(32):
            row = (head // 4) * 16 + t * 4 + head % 4
            qd[pl.ds(row, 32, stride=128), :] = dq[t, :, head * HD : (head + 1) * HD].astype(jnp.float32)

    remote(theirs, theirs, kv_send.at[3], kv_recv.at[3], x * 4 + my, g).wait_recv()
    for i, gg in enumerate(z_peers):
        z_copies.append(remote(theirs, theirs, kv_send.at[7 + i], kv_recv.at[7 + i], c, gg))
        z_copies[-1].start()
    whole = kv.at[:, :, g]
    sib_copies = [remote(whole, whole, kv_send.at[10], kv_recv.at[10], c, sib)]
    sib_copies[0].start()

    loads[3].wait()
    lane = lax.broadcasted_iota(jnp.int32, (128, 128), 1)

    def request(r, unused):
        kvr = jnp.concatenate([pool[table_ref[r, j]] for j in range(4)], axis=0)
        q = qd[pl.ds(pl.multiple_of(r * 128, 128), 128), :].astype(jnp.bfloat16)
        s = jnp.concatenate(
            [
                lax.dot_general(
                    q[h * 32 : (h + 1) * 32], kvr[:, h * 256 : h * 256 + 128],
                    (((1,), (1,)), ((), ())), preferred_element_type=jnp.float32,
                )
                for h in range(4)
            ],
            axis=0,
        )
        ok = lane + c * 128 < len_ref[r]
        s = jnp.where(ok, s, NEG)
        m = jnp.max(s, axis=1, keepdims=True)
        p = jnp.where(ok, jnp.exp2((s - m) * EXP2), 0.0)
        l = jnp.sum(p, axis=1, keepdims=True)
        pb = p.astype(jnp.bfloat16)
        for h in range(4):
            pv = jnp.dot(
                pb[h * 32 : (h + 1) * 32], kvr[:, h * 256 + 128 : h * 256 + 256], preferred_element_type=jnp.float32
            ).astype(jnp.bfloat16)
            here = pl.ds(pl.multiple_of(r * 16, 16), 16)
            dec_send[2 * h, here, :] = pv[:16]
            dec_send[2 * h + 1, here, :] = pv[16:]
        stat_send[...] = jnp.where(lane == r, m, jnp.where(lane == r + 32, l, stat_send[...]))
        return unused

    stat_send[...] = jnp.zeros_like(stat_send)
    lax.fori_loop(0, 32, request, 0)

    for i, gg in enumerate(z_from):
        for part, base in ((kv.at[:, pl.ds(2 * py, 2), gg], 4), (kv.at[:, pl.ds(2 - 2 * py, 2), gg], 7)):
            remote(part, part, kv_send.at[base + i], kv_recv.at[base + i], c, gg).wait_recv()
        whole = kv.at[:, :, gg]
        sib_copies.append(remote(whole, whole, kv_send.at[11 + i], kv_recv.at[11 + i], c, sib))
        sib_copies[-1].start()

    dec_copies = []
    for i in range(1, 8):
        cc = (c + i) % 8
        dec_copies.append(remote(dec_send.at[cc], dec_recv.at[i], d_send.at[i], d_recv.at[i], cc, g))
        dec_copies.append(
            remote(
                stat_send.at[pl.ds(pl.multiple_of(cc * 16, 16), 16)], stat_recv.at[i], s_send.at[i], s_recv.at[i], cc, g
            )
        )
    for copy in dec_copies:
        copy.start()

    loads[2].wait()
    dests = [dest_ref[p, 0] for p in range(4)]
    ranks = [sum([(dests[q] == dests[p]).astype(jnp.int32) for q in range(p)], jnp.int32(0)) for p in range(4)]
    marks = [dests[p] * 2 + ranks[p] for p in range(4)]

    def slot_page(i, unused):
        page = jnp.zeros((32, 1024), jnp.bfloat16)
        for p in range(4):
            hit = jnp.full((32, 1024), marks[p], jnp.int32) == i
            page = jnp.where(hit, pages[p * 32 : (p + 1) * 32, :], page)
        arr_send[i] = page
        return unused

    lax.fori_loop(0, 16, slot_page, 0)
    arr_copies = []
    for i in range(1, 8):
        gg = (g + i) % 8
        arr_copies.append(
            remote(arr_send.at[pl.ds(2 * gg, 2)], arr_ref.at[pl.ds(2 * g, 2)], a_send.at[i], a_recv.at[i], c, gg)
        )
        arr_copies[-1].start()
    own_arr = pltpu.make_async_copy(arr_send.at[pl.ds(2 * g, 2)], arr_ref.at[pl.ds(2 * g, 2)], local_sem.at[6])
    own_arr.start()

    own_q.wait()
    for i, (cc, gg, kk) in enumerate(q_peers):
        remote(qin.at[i], qin.at[i], q_send.at[i], q_recv.at[i], cc, gg).wait_recv()
    for i, gg in enumerate([sib] + [((z + 4 - d) % 4) * 2 + 1 - co for d in (1, 3, 2)]):
        whole = kv.at[:, :, gg]
        remote(whole, whole, kv_send.at[10 + i], kv_recv.at[10 + i], c, sib).wait_recv()

    row = lax.broadcasted_iota(jnp.int32, (CHAIN, 1024), 0) % 128
    col = lax.broadcasted_iota(jnp.int32, (CHAIN, 1024), 1)
    gap = col - row
    nchain = 1024 // CHAIN
    per = CHAIN // HD

    def prompt_slot(slot, unused):
        cs = jnp.where(slot == 0, c_a, jnp.where(slot == 1, c_b, jnp.where(slot == 2, c_c, c)))
        gs = jnp.where((slot == 1) | (slot == 2), gm, g)
        qs = [
            jnp.concatenate([qin[slot, :, (i * per + j) * HD : (i * per + j + 1) * HD] for j in range(per)], axis=0)
            for i in range(nchain)
        ]

        def chunk(cc):
            both = kv[cc // 4, cc % 4].reshape(1024, 256)
            return both[:, :HD], both[:, HD:]

        def full(cc, states):
            return flash_chunk(qs, *chunk(cc), states, None)

        start = tuple(
            (
                jnp.full((CHAIN, 1), NEG, jnp.float32),
                jnp.zeros((CHAIN, HD), jnp.float32),
                jnp.zeros((CHAIN, HD), jnp.float32),
            )
            for i in range(nchain)
        )
        states = lax.fori_loop(0, cs, full, start)
        states = flash_chunk(qs, *chunk(cs), states, gap <= gs * 128)
        for i in range(nchain):
            m, l, acc = states[i]
            o = (acc / jnp.sum(l, axis=1, keepdims=True)).astype(jnp.bfloat16)
            for j in range(per):
                obuf[slot, :, (i * per + j) * HD : (i * per + j + 1) * HD] = o[j * HD : (j + 1) * HD]
        return unused

    lax.fori_loop(0, 4, prompt_slot, 0)
    columns = pl.ds(pl.multiple_of(k * 1024, 1024), 1024)
    own_out = pltpu.make_async_copy(obuf.at[3], out_ref.at[:, columns], local_sem.at[7])
    own_out.start()
    o_copies = []
    for i, (cc, gg, kk) in enumerate(q_peers):
        o_copies.append(remote(obuf.at[i], out_ref.at[:, columns], o_send.at[i], o_recv.at[i], cc, gg))
        o_copies[-1].start()

    loads[1].wait()
    for i in range(1, 8):
        remote(dec_recv.at[i], dec_recv.at[i], d_send.at[i], d_recv.at[i], c, g).wait_recv()
        remote(stat_recv.at[i], stat_recv.at[i], s_send.at[i], s_recv.at[i], c, g).wait_recv()
    h = c // 2
    q = jnp.concatenate(
        [qd[pl.ds(pl.multiple_of(r * 128 + c * 16, 16), 16), :] for r in range(32)], axis=0
    ).astype(jnp.bfloat16)
    knew = dn[:, :, pl.ds(pl.multiple_of(h * 256, 256), 128)].reshape(128, 128)
    vnew = dn[:, :, pl.ds(pl.multiple_of(h * 256 + 128, 128), 128)].reshape(128, 128)
    s = lax.dot_general(q, knew, (((1,), (1,)), ((), ())), preferred_element_type=jnp.float32)
    drow = lax.broadcasted_iota(jnp.int32, (512, 128), 0)
    dcol = lax.broadcasted_iota(jnp.int32, (512, 128), 1)
    same = dcol % 32 == drow // 16
    ok = same & (dcol // 32 <= (drow % 16) // 4)
    s = jnp.where(ok, s, NEG)
    m_new = jnp.max(s, axis=1, keepdims=True)
    p = jnp.where(ok, jnp.exp2((s - m_new) * EXP2), 0.0)
    l_new = jnp.sum(p, axis=1, keepdims=True)
    o_new = jnp.dot(p.astype(jnp.bfloat16), vnew, preferred_element_type=jnp.float32)

    at_m = dcol == drow // 16
    at_l = dcol == drow // 16 + 32
    new_stat = jnp.sum(
        (jnp.where(at_m, m_new, 0.0) + jnp.where(at_l, l_new, 0.0)).reshape(32, 16, 128), axis=0
    )
    stats = [new_stat, stat_send[pl.ds(pl.multiple_of(c * 16, 16), 16), :]] + [stat_recv[i] for i in range(1, 8)]
    tops = [stat[:, 0:32] for stat in stats]
    sums = [stat[:, 32:64] for stat in stats]
    top = tops[0]
    for other in tops[1:]:
        top = jnp.maximum(top, other)
    fixes = [jnp.exp2((other - top) * EXP2) for other in tops]
    total = fixes[0] * sums[0]
    for fix, part in zip(fixes[1:], sums[1:]):
        total = total + fix * part
    spread = dcol[:, 0:32] == drow[:, 0:32] // 16
    result = None
    for i, fix in enumerate(fixes):
        weight = jnp.sum(
            jnp.where(spread, jnp.concatenate([fix / total] * 32, axis=0), 0.0), axis=1, keepdims=True
        )
        part = o_new if i == 0 else (dec_send[c] if i == 1 else dec_recv[i - 1]).astype(jnp.float32)
        result = part * weight if result is None else result + part * weight
    fin[...] = result
    for t in range(4):
        for j in range(4):
            finb[t, :, j * HD : (j + 1) * HD] = fin[pl.ds(t * 4 + j, 32, stride=16), :].astype(jnp.bfloat16)
    dcols = pl.ds(pl.multiple_of(c * 512, 512), 512)
    own_dec = pltpu.make_async_copy(finb, dec_ref.at[:, :, dcols], local_sem.at[8])
    own_dec.start()
    f_copies = []
    for i in range(1, 8):
        f_copies.append(
            remote(finb, dec_ref.at[:, :, dcols], f_send.at[i], f_recv.at[i], (c + i) % 8, g)
        )
        f_copies[-1].start()

    for i in range(1, 8):
        gg = (g + 8 - i) % 8
        here = arr_ref.at[pl.ds(2 * gg, 2)]
        remote(here, here, a_send.at[i], a_recv.at[i], c, gg).wait_recv()
        cc = (c + 8 - i) % 8
        here = dec_ref.at[:, :, pl.ds(pl.multiple_of(cc * 512, 512), 512)]
        remote(here, here, f_send.at[i], f_recv.at[i], cc, g).wait_recv()
    for i, (cc, gg, kk) in enumerate(q_peers):
        here = out_ref.at[:, pl.ds(pl.multiple_of(kk * 1024, 1024), 1024)]
        remote(here, here, o_send.at[i], o_recv.at[i], cc, gg).wait_recv()
    for copy in kv_first + [y_copy] + z_copies + sib_copies + q_copies + dec_copies + arr_copies + o_copies + f_copies:
        copy.wait_send()
    own_arr.wait()
    own_out.wait()
    own_dec.wait()


def on_device(prefill_query, prefill_kv, page_dest, cache_pool, page_table, context_len, dec_query, dec_new):
    any_spec, smem = pl.BlockSpec(memory_space=pl.ANY), pl.BlockSpec(memory_space=pltpu.SMEM)
    bf16, f32 = jnp.bfloat16, jnp.float32
    dma = pltpu.SemaphoreType.DMA
    out, arrivals, dec = pl.pallas_call(
        kernel,
        out_shape=(
            jax.ShapeDtypeStruct((128, 4096), bf16),
            jax.ShapeDtypeStruct((16, 32, 1024), bf16),
            jax.ShapeDtypeStruct((4, 32, 4096), bf16),
        ),
        in_specs=[any_spec, any_spec, smem, any_spec, smem, smem, any_spec, any_spec],
        out_specs=(any_spec, any_spec, any_spec),
        scratch_shapes=[
            pltpu.VMEM((2, 4, 8, 128, 256), bf16),
            pltpu.VMEM((4, 128, 1024), bf16),
            pltpu.VMEM((4, 128, 1024), bf16),
            pltpu.VMEM((128, 1024), bf16),
            pltpu.VMEM((16, 32, 1024), bf16),
            pltpu.VMEM((128, 32, 1024), bf16),
            pltpu.VMEM((4, 32, 4096), bf16),
            pltpu.VMEM((4, 32, 1024), bf16),
            pltpu.VMEM((32 * 128, 128), f32),
            pltpu.VMEM((8, 512, 128), bf16),
            pltpu.VMEM((128, 128), f32),
            pltpu.VMEM((8, 512, 128), bf16),
            pltpu.VMEM((8, 16, 128), f32),
            pltpu.VMEM((512, 128), f32),
            pltpu.VMEM((4, 32, 512), bf16),
            dma((9,)),
            dma((3,)), dma((3,)), dma((14,)), dma((14,)), dma((3,)), dma((3,)),
            dma((8,)), dma((8,)), dma((8,)), dma((8,)), dma((8,)), dma((8,)), dma((8,)), dma((8,)),
        ],
        compiler_params=pltpu.CompilerParams(
            collective_id=0, has_side_effects=True, vmem_limit_bytes=58 * 2**20
        ),
        cost_estimate=pl.CostEstimate(flops=10**10, bytes_accessed=20 * 2**20, transcendentals=2 * 10**7),
        name="serving_step",
    )(
        prefill_query, prefill_kv, page_dest, cache_pool.reshape(128, 32, 1024), page_table, context_len,
        dec_query, dec_new,
    )
    return out, arrivals.reshape(1, 1, 16, 32, 1024), dec


def solution(mesh):
    placed = (
        P(("ctx", "grp"), "head"),
        P(("ctx", "grp"), "head"),
        P(("ctx", "grp"), None),
        P("ctx", "grp", None, None, "head"),
        P("grp", "ctx"),
        P("grp"),
        P(None, "grp", "head"),
        P(None, "grp", "head"),
    )
    return jax.shard_map(
        on_device,
        mesh=mesh,
        in_specs=placed,
        out_specs=(
            P(("ctx", "grp"), "head"),
            P("grp", "ctx", None, None, "head"),
            P(None, "grp", "head"),
        ),
        check_vma=False,
    )
```

```python
import jax
import jax.numpy as jnp
from jax import lax
from jax.experimental import pallas as pl
from jax.experimental.pallas import tpu as pltpu
from jax.sharding import PartitionSpec as P

HD = 128
NEG = -1e30
SCALE = HD**-0.5
EXP2 = SCALE * 1.4426950408889634
MESH = pl.DeviceIdType.MESH
CHAIN = 256


def softmax_step(s, v, state):
    m, l, acc = state
    mn = jnp.maximum(m, jnp.max(s, axis=1, keepdims=True))
    al = jnp.exp2((m - mn) * EXP2)
    p = jnp.exp2((s - mn) * EXP2)
    part = p[:, 0:HD]
    for t in range(1, s.shape[1] // HD):
        part = part + p[:, t * HD : (t + 1) * HD]
    acc = acc * al + jnp.dot(p.astype(jnp.bfloat16), v, preferred_element_type=jnp.float32)
    return mn, l * al + part, acc


def flash_chunk(qs, k, v, states, allowed):
    def score(q):
        s = lax.dot_general(q, k, (((1,), (1,)), ((), ())), preferred_element_type=jnp.float32)
        return s if allowed is None else jnp.where(allowed, s, NEG)

    out = []
    s = score(qs[0])
    for i in range(len(qs)):
        following = score(qs[i + 1]) if i + 1 < len(qs) else None
        out.append(softmax_step(s, v, states[i]))
        s = following
    return tuple(out)


def kernel(
    pq_ref, pkv_ref, dest_ref, pool_ref, table_ref, len_ref, dq_ref, dn_ref,
    out_ref, arr_ref, dec_ref,
    kv, qin, obuf, pages, arr_send, pool, dq, dn, qd, dec_send, stat_send, dec_recv, stat_recv, fin, finb,
    st_m, st_l, st_acc,
    local_sem, q_send, q_recv, kv_send, kv_recv, o_send, o_recv, a_send, a_recv,
    d_send, d_recv, s_send, s_recv, f_send, f_recv,
):
    c, g = lax.axis_index("ctx"), lax.axis_index("grp")
    x, y, z, co = c // 4, c % 4, g // 2, g % 2
    py = y // 2
    hy = (y % 2 + py) % 2
    k = x * 2 + hy
    ox = 1 - x
    yx = y + 1 - 2 * (y % 2)
    my = 3 - y
    myx = my + 1 - 2 * (my % 2)
    sib = z * 2 + 1 - co

    c_a, c_b, c_c = x * 4 + yx, ox * 4 + my, ox * 4 + myx
    q_peers = [(c_a, x * 2 + 1 - hy), (c_b, ox * 2 + hy), (c_c, ox * 2 + 1 - hy)]
    kv_peers = [(c_a, x * 2 + 1 - hy), (ox * 4 + y, ox * 2 + hy), (ox * 4 + yx, ox * 2 + 1 - hy)]

    def remote(src, dst, send, recv, cc, gg):
        return pltpu.make_async_remote_copy(
            src_ref=src, dst_ref=dst, send_sem=send, recv_sem=recv,
            device_id={"ctx": cc, "grp": gg}, device_id_type=MESH,
        )

    loads = [
        pltpu.make_async_copy(dq_ref, dq, local_sem.at[0]),
        pltpu.make_async_copy(pool_ref, pool, local_sem.at[3]),
        pltpu.make_async_copy(dn_ref, dn, local_sem.at[1]),
        pltpu.make_async_copy(pkv_ref, pages, local_sem.at[2]),
    ]
    own_q = pltpu.make_async_copy(pq_ref.at[:, pl.ds(pl.multiple_of(k * 1024, 1024), 1024)], qin.at[3], local_sem.at[4])
    own_kv = pltpu.make_async_copy(pkv_ref.at[:, pl.ds(pl.multiple_of(k * 256, 256), 256)], kv.at[x, y, g], local_sem.at[5])
    own_kv.start()
    for load in loads:
        load.start()
    own_q.start()

    barrier = pltpu.get_barrier_semaphore()
    partners = [((c + i) % 8, g) for i in range(1, 8)] + [(c, (g + i) % 8) for i in range(1, 8)]
    for cc, gg in partners:
        pl.semaphore_signal(barrier, inc=1, device_id={"ctx": cc, "grp": gg}, device_id_type=MESH)
    pl.semaphore_wait(barrier, len(partners))

    hops = (1, 3, 2)
    z_peers = [((z + d) % 4) * 2 + co for d in hops]
    z_from = [((z + 4 - d) % 4) * 2 + co for d in hops]
    s_from = [((z + 4 - d) % 4) * 2 + 1 - co for d in hops]
    mirror = x * 4 + my
    own_pieces = [c] + [cc for cc, kk in kv_peers]
    mirror_pieces = [mirror, x * 4 + myx, ox * 4 + my, ox * 4 + myx]
    hop_copies = []

    def piece(cc, gg):
        return kv.at[cc // 4, cc % 4, gg]

    def half(first, gg):
        return kv.at[:, pl.ds(2 * py if first else 2 - 2 * py, 2), gg]

    def send_on(src, at, cc, gg):
        hop_copies.append(remote(src, src, kv_send.at[at], kv_recv.at[at], cc, gg))
        hop_copies[-1].start()

    def arrived(src, at, cc, gg):
        remote(src, src, kv_send.at[at], kv_recv.at[at], cc, gg).wait_recv()

    def pass_on(p):
        here = piece(own_pieces[p], g)
        for i, gg in enumerate(z_peers):
            send_on(here, 7 + 3 * p + i, c, gg)
        send_on(here, 3 + p, mirror, g)
        send_on(here, 19 + p, c, sib)

    kv_first = []
    for i, (cc, kk) in enumerate(kv_peers):
        kv_first.append(
            remote(pkv_ref.at[:, pl.ds(pl.multiple_of(kk * 256, 256), 256)], piece(c, g), kv_send.at[i], kv_recv.at[i], cc, g)
        )
        kv_first[-1].start()
    own_kv.wait()
    pass_on(0)
    q_copies = []
    for i, (cc, kk) in enumerate(q_peers):
        q_copies.append(
            remote(pq_ref.at[:, pl.ds(pl.multiple_of(kk * 1024, 1024), 1024)], qin.at[i], q_send.at[i], q_recv.at[i], cc, g)
        )
        q_copies[-1].start()

    loads[0].wait()
    for t in range(4):
        for head in range(32):
            row = (head // 4) * 16 + t * 4 + head % 4
            qd[pl.ds(row, 32, stride=128), :] = dq[t, :, head * HD : (head + 1) * HD].astype(jnp.float32)

    for p in range(1, 4):
        arrived(piece(own_pieces[p], g), p - 1, own_pieces[p], g)
        pass_on(p)

    loads[1].wait()
    lane = lax.broadcasted_iota(jnp.int32, (128, 128), 1)
    stat_send[...] = jnp.zeros_like(stat_send)
    together = 4

    def requests(n, unused):
        numbers = [n * together + i for i in range(together)]
        kvs, scores = [], []
        for r in numbers:
            kvr = jnp.concatenate([pool[table_ref[j, r]] for j in range(4)], axis=0)
            q = qd[pl.ds(pl.multiple_of(r * 128, 128), 128), :].astype(jnp.bfloat16)
            s = jnp.concatenate(
                [
                    lax.dot_general(
                        q[h * 32 : (h + 1) * 32], kvr[:, h * 256 : h * 256 + 128],
                        (((1,), (1,)), ((), ())), preferred_element_type=jnp.float32,
                    )
                    for h in range(4)
                ],
                axis=0,
            )
            kvs.append(kvr)
            scores.append(s)
        oks = [lane + c * 128 < len_ref[r] for r in numbers]
        scores = [jnp.where(ok, s, NEG) for ok, s in zip(oks, scores)]
        tops = [jnp.max(s, axis=1, keepdims=True) for s in scores]
        expos = [jnp.where(ok, jnp.exp2((s - m) * EXP2), 0.0) for ok, s, m in zip(oks, scores, tops)]
        sums = [jnp.sum(p, axis=1, keepdims=True) for p in expos]
        stat = stat_send[...]
        for r, m, l in zip(numbers, tops, sums):
            stat = jnp.where(lane == r, m, jnp.where(lane == r + 32, l, stat))
        stat_send[...] = stat
        for r, kvr, p in zip(numbers, kvs, expos):
            pb = p.astype(jnp.bfloat16)
            for h in range(4):
                pv = jnp.dot(
                    pb[h * 32 : (h + 1) * 32], kvr[:, h * 256 + 128 : h * 256 + 256], preferred_element_type=jnp.float32
                ).astype(jnp.bfloat16)
                here = pl.ds(pl.multiple_of(r * 16, 16), 16)
                dec_send[2 * h, here, :] = pv[:16]
                dec_send[2 * h + 1, here, :] = pv[16:]
        return unused

    lax.fori_loop(0, 16 // together, requests, 0)
    lax.fori_loop(16 // together, 32 // together, requests, 0)

    dec_copies = []
    for i in range(1, 8):
        cc = (c + i) % 8
        dec_copies.append(remote(dec_send.at[cc], dec_recv.at[i], d_send.at[i], d_recv.at[i], cc, g))
        dec_copies.append(
            remote(
                stat_send.at[pl.ds(pl.multiple_of(cc * 16, 16), 16)], stat_recv.at[i], s_send.at[i], s_recv.at[i], cc, g
            )
        )
    for p in range(4):
        for i, gg in enumerate(z_from):
            here = piece(own_pieces[p], gg)
            arrived(here, 7 + 3 * p + i, c, gg)
            send_on(here, 23 + 3 * p + i, c, sib)
    for p in range(4):
        arrived(piece(mirror_pieces[p], g), 3 + p, mirror, g)
    for i, gg in enumerate(z_peers):
        send_on(half(False, g), 35 + i, c, gg)
    send_on(half(False, g), 38, c, sib)

    for copy in dec_copies:
        copy.start()

    loads[3].wait()
    dests = [dest_ref[0, p] for p in range(4)]
    ranks = [sum([(dests[q] == dests[p]).astype(jnp.int32) for q in range(p)], jnp.int32(0)) for p in range(4)]
    marks = [dests[p] * 2 + ranks[p] for p in range(4)]

    def slot_page(i, unused):
        page = jnp.zeros((32, 1024), jnp.bfloat16)
        for p in range(4):
            hit = jnp.full((32, 1024), marks[p], jnp.int32) == i
            page = jnp.where(hit, pages[p * 32 : (p + 1) * 32, :], page)
        arr_send[i] = page
        return unused

    lax.fori_loop(0, 16, slot_page, 0)

    row = lax.broadcasted_iota(jnp.int32, (CHAIN, 1024), 0) % 128
    col = lax.broadcasted_iota(jnp.int32, (CHAIN, 1024), 1)
    allowed = col - row <= g * 128
    nchain = 1024 // CHAIN
    per = CHAIN // HD
    columns = pl.ds(pl.multiple_of(k * 1024, 1024), 1024)

    def queries_of(slot):
        return [
            jnp.concatenate([qin[slot, :, (i * per + j) * HD : (i * per + j + 1) * HD] for j in range(per)], axis=0)
            for i in range(nchain)
        ]

    def chunk(cc):
        both = kv[cc // 4, cc % 4].reshape(1024, 256)
        return both[:, :HD], both[:, HD:]

    def over(qs, first, cs, states):
        pair = 2 * py if first else 2 - 2 * py
        ids = [(j // 2) * 4 + pair + j % 2 for j in range(4)]
        count = sum([(one < cs).astype(jnp.int32) for one in ids], jnp.int32(0))

        def full(j, held):
            return flash_chunk(qs, *chunk((j // 2) * 4 + pair + j % 2), held, None)

        return lax.fori_loop(0, count, full, states)

    def fresh():
        return tuple(
            (
                jnp.full((CHAIN, 1), NEG, jnp.float32),
                jnp.zeros((CHAIN, HD), jnp.float32),
                jnp.zeros((CHAIN, HD), jnp.float32),
            )
            for i in range(nchain)
        )

    def keep(slot, states):
        for i in range(nchain):
            here = pl.ds(i * CHAIN, CHAIN)
            m, l, acc = states[i]
            st_m[slot, here, :] = jnp.broadcast_to(m, (CHAIN, HD))
            st_l[slot, here, :] = l
            st_acc[slot, here, :] = acc

    def kept(slot):
        states = []
        for i in range(nchain):
            here = pl.ds(i * CHAIN, CHAIN)
            states.append((st_m[slot, here, 0:1], st_l[slot, here, :], st_acc[slot, here, :]))
        return tuple(states)

    def finish(slot, states):
        for i in range(nchain):
            m, l, acc = states[i]
            o = (acc / jnp.sum(l, axis=1, keepdims=True)).astype(jnp.bfloat16)
            for j in range(per):
                obuf[slot, :, (i * per + j) * HD : (i * per + j + 1) * HD] = o[j * HD : (j + 1) * HD]

    def pick(j):
        slot = jnp.where(j == 0, 0, jnp.where(j == 1, 3, jnp.where(j == 2, 2, 1)))
        return slot, jnp.where(j == 0, c_a, jnp.where(j == 1, c, jnp.where(j == 2, c_c, c_b)))

    def masked(qs, cs, wanted, states):
        def last(j, held):
            return flash_chunk(qs, *chunk(cs), held, allowed)

        return lax.fori_loop(0, wanted.astype(jnp.int32), last, states)

    def first_pass(j, unused):
        slot, cs = pick(j)

        @pl.when(j != 1)
        def _():
            remote(qin.at[slot], qin.at[slot], q_send.at[slot], q_recv.at[slot], cs, g).wait_recv()

        qs = queries_of(slot)
        states = over(qs, True, cs, fresh())
        keep(slot, masked(qs, cs, j == 0, states))
        return unused

    def second_pass(n, unused):
        j = (n + 2) % 4
        slot, cs = pick(j)
        qs = queries_of(slot)
        states = over(qs, False, cs, kept(slot))
        finish(slot, masked(qs, cs, j != 0, states))

        @pl.when(j != 1)
        def _():
            remote(obuf.at[slot], out_ref.at[:, columns], o_send.at[slot], o_recv.at[slot], cs, g).start()

        return unused

    own_q.wait()
    for p in range(4):
        arrived(piece(own_pieces[p], sib), 19 + p, c, sib)
        for i, gg in enumerate(s_from):
            arrived(piece(own_pieces[p], gg), 23 + 3 * p + i, c, sib)
    lax.fori_loop(0, 4, first_pass, 0)

    for i, gg in enumerate(z_from):
        arrived(half(False, gg), 35 + i, c, gg)
        send_on(half(False, gg), 39 + i, c, sib)
    arr_copies = []
    for i in range(1, 8):
        gg = (g + i) % 8
        arr_copies.append(
            remote(arr_send.at[pl.ds(2 * gg, 2)], arr_ref.at[pl.ds(2 * g, 2)], a_send.at[i], a_recv.at[i], c, gg)
        )
        arr_copies[-1].start()
    own_arr = pltpu.make_async_copy(arr_send.at[pl.ds(2 * g, 2)], arr_ref.at[pl.ds(2 * g, 2)], local_sem.at[6])
    own_arr.start()

    loads[2].wait()
    for i in range(1, 8):
        remote(dec_recv.at[i], dec_recv.at[i], d_send.at[i], d_recv.at[i], c, g).wait_recv()
        remote(stat_recv.at[i], stat_recv.at[i], s_send.at[i], s_recv.at[i], c, g).wait_recv()
    h = c // 2
    q = jnp.concatenate(
        [qd[pl.ds(pl.multiple_of(r * 128 + c * 16, 16), 16), :] for r in range(32)], axis=0
    ).astype(jnp.bfloat16)
    knew = dn[:, :, pl.ds(pl.multiple_of(h * 256, 256), 128)].reshape(128, 128)
    vnew = dn[:, :, pl.ds(pl.multiple_of(h * 256 + 128, 128), 128)].reshape(128, 128)
    s = lax.dot_general(q, knew, (((1,), (1,)), ((), ())), preferred_element_type=jnp.float32)
    drow = lax.broadcasted_iota(jnp.int32, (512, 128), 0)
    dcol = lax.broadcasted_iota(jnp.int32, (512, 128), 1)
    ok = (dcol % 32 == drow // 16) & (dcol // 32 <= (drow % 16) // 4)
    s = jnp.where(ok, s, NEG)
    m_new = jnp.max(s, axis=1, keepdims=True)
    p = jnp.where(ok, jnp.exp2((s - m_new) * EXP2), 0.0)
    l_new = jnp.sum(p, axis=1, keepdims=True)
    o_new = jnp.dot(p.astype(jnp.bfloat16), vnew, preferred_element_type=jnp.float32)

    new_stat = jnp.sum(
        jnp.where(dcol == drow // 16, m_new, jnp.where(dcol == drow // 16 + 32, l_new, 0.0)).reshape(32, 16, 128), axis=0
    )
    stats = [new_stat, stat_send[pl.ds(pl.multiple_of(c * 16, 16), 16), :]] + [stat_recv[i] for i in range(1, 8)]
    tops = [stat[:, 0:32] for stat in stats]
    sums = [stat[:, 32:64] for stat in stats]
    top = tops[0]
    for other in tops[1:]:
        top = jnp.maximum(top, other)
    fixes = [jnp.exp2((other - top) * EXP2) for other in tops]
    total = fixes[0] * sums[0]
    for fix, part in zip(fixes[1:], sums[1:]):
        total = total + fix * part
    spread = dcol[:, 0:32] == drow[:, 0:32] // 16
    result = None
    for i, fix in enumerate(fixes):
        weight = jnp.sum(
            jnp.where(spread, jnp.concatenate([fix / total] * 32, axis=0), 0.0), axis=1, keepdims=True
        )
        part = o_new if i == 0 else (dec_send[c] if i == 1 else dec_recv[i - 1]).astype(jnp.float32)
        result = part * weight if result is None else result + part * weight
    fin[...] = result
    for t in range(4):
        for j in range(4):
            finb[t, :, j * HD : (j + 1) * HD] = fin[pl.ds(t * 4 + j, 32, stride=16), :].astype(jnp.bfloat16)
    dcols = pl.ds(pl.multiple_of(c * 512, 512), 512)
    own_dec = pltpu.make_async_copy(finb, dec_ref.at[:, :, dcols], local_sem.at[8])
    own_dec.start()
    f_copies = []
    for i in range(1, 8):
        f_copies.append(
            remote(finb, dec_ref.at[:, :, dcols], f_send.at[i], f_recv.at[i], (c + i) % 8, g)
        )
        f_copies[-1].start()

    arrived(half(False, sib), 38, c, sib)
    for i, gg in enumerate(s_from):
        arrived(half(False, gg), 39 + i, c, sib)
    lax.fori_loop(0, 4, second_pass, 0)
    own_out = pltpu.make_async_copy(obuf.at[3], out_ref.at[:, columns], local_sem.at[7])
    own_out.start()

    for i in range(1, 8):
        gg = (g + 8 - i) % 8
        here = arr_ref.at[pl.ds(2 * gg, 2)]
        remote(here, here, a_send.at[i], a_recv.at[i], c, gg).wait_recv()
        cc = (c + 8 - i) % 8
        here = dec_ref.at[:, :, pl.ds(pl.multiple_of(cc * 512, 512), 512)]
        remote(here, here, f_send.at[i], f_recv.at[i], cc, g).wait_recv()
    for i, (cc, kk) in enumerate(q_peers):
        here = out_ref.at[:, pl.ds(pl.multiple_of(kk * 1024, 1024), 1024)]
        remote(obuf.at[i], here, o_send.at[i], o_recv.at[i], cc, g).wait()
    for copy in kv_first + hop_copies + q_copies + dec_copies + arr_copies + f_copies:
        copy.wait_send()
    own_arr.wait()
    own_out.wait()
    own_dec.wait()


def hand_out(out_in, arr_in, dec_in, out_ref, arr_ref, dec_ref, out_buf, arr_buf, dec_buf, sem_in, sem_out):
    moves = []
    for src, buf, dst in ((out_in, out_buf, out_ref), (arr_in, arr_buf, arr_ref), (dec_in, dec_buf, dec_ref)):
        rows = src.shape[0] // 4
        for i in range(4):
            here = pl.ds(i * rows, rows)
            n = len(moves)
            moves.append(
                (
                    pltpu.make_async_copy(src.at[here], buf.at[here], sem_in.at[n]),
                    pltpu.make_async_copy(buf.at[here], dst.at[here], sem_out.at[n]),
                )
            )
    for load, store in moves:
        load.start()
    for load, store in moves:
        load.wait()
        store.start()
    for load, store in moves:
        store.wait()


def on_device(prefill_query, prefill_kv, page_dest, cache_pool, page_table, context_len, dec_query, dec_new):
    any_spec, smem = pl.BlockSpec(memory_space=pl.ANY), pl.BlockSpec(memory_space=pltpu.SMEM)
    bf16, f32 = jnp.bfloat16, jnp.float32
    dma = pltpu.SemaphoreType.DMA
    out, arrivals, dec = pl.pallas_call(
        kernel,
        out_shape=(
            jax.ShapeDtypeStruct((128, 4096), bf16),
            jax.ShapeDtypeStruct((16, 32, 1024), bf16),
            jax.ShapeDtypeStruct((4, 32, 4096), bf16),
        ),
        in_specs=[any_spec, any_spec, smem, any_spec, smem, smem, any_spec, any_spec],
        out_specs=(any_spec, any_spec, any_spec),
        scratch_shapes=[
            pltpu.VMEM((2, 4, 8, 128, 256), bf16),
            pltpu.VMEM((4, 128, 1024), bf16),
            pltpu.VMEM((4, 128, 1024), bf16),
            pltpu.VMEM((128, 1024), bf16),
            pltpu.VMEM((16, 32, 1024), bf16),
            pltpu.VMEM((128, 32, 1024), bf16),
            pltpu.VMEM((4, 32, 4096), bf16),
            pltpu.VMEM((4, 32, 1024), bf16),
            pltpu.VMEM((32 * 128, 128), f32),
            pltpu.VMEM((8, 512, 128), bf16),
            pltpu.VMEM((128, 128), f32),
            pltpu.VMEM((8, 512, 128), bf16),
            pltpu.VMEM((8, 16, 128), f32),
            pltpu.VMEM((512, 128), f32),
            pltpu.VMEM((4, 32, 512), bf16),
            pltpu.VMEM((4, 1024, 128), f32),
            pltpu.VMEM((4, 1024, 128), f32),
            pltpu.VMEM((4, 1024, 128), f32),
            dma((9,)),
            dma((3,)), dma((3,)), dma((42,)), dma((42,)), dma((3,)), dma((3,)),
            dma((8,)), dma((8,)), dma((8,)), dma((8,)), dma((8,)), dma((8,)), dma((8,)), dma((8,)),
        ],
        compiler_params=pltpu.CompilerParams(
            collective_id=0, has_side_effects=True, vmem_limit_bytes=58 * 2**20
        ),
        cost_estimate=pl.CostEstimate(flops=10**10, bytes_accessed=20 * 2**20, transcendentals=2 * 10**7),
        name="serving_step",
    )(
        prefill_query, prefill_kv, page_dest.T, cache_pool.reshape(128, 32, 1024), page_table.T, context_len,
        dec_query, dec_new,
    )
    out, arrivals, dec = pl.pallas_call(
        hand_out,
        out_shape=tuple(jax.ShapeDtypeStruct(a.shape, a.dtype) for a in (out, arrivals, dec)),
        in_specs=[pl.BlockSpec(memory_space=pltpu.HBM)] * 3,
        out_specs=(pl.BlockSpec(memory_space=pltpu.HBM),) * 3,
        scratch_shapes=[pltpu.VMEM(a.shape, a.dtype) for a in (out, arrivals, dec)] + [dma((12,)), dma((12,))],
        cost_estimate=pl.CostEstimate(flops=0, bytes_accessed=6 * 2**20, transcendentals=0),
        name="hand_out",
    )(out, arrivals, dec)
    return out, arrivals.reshape(1, 1, 16, 32, 1024), dec


def solution(mesh):
    placed = (
        P(("ctx", "grp"), "head"),
        P(("ctx", "grp"), "head"),
        P(("ctx", "grp"), None),
        P("ctx", "grp", None, None, "head"),
        P("grp", "ctx"),
        P("grp"),
        P(None, "grp", "head"),
        P(None, "grp", "head"),
    )
    return jax.shard_map(
        on_device,
        mesh=mesh,
        in_specs=placed,
        out_specs=(
            P(("ctx", "grp"), "head"),
            P("grp", "ctx", None, None, "head"),
            P(None, "grp", "head"),
        ),
        check_vma=False,
    )
```

```python
import jax
import jax.numpy as jnp
from jax import lax
from jax.experimental import pallas as pl
from jax.experimental.pallas import tpu as pltpu
from jax.sharding import PartitionSpec as P

HD = 128
NEG = -1e30
SCALE = HD**-0.5
EXP2 = SCALE * 1.4426950408889634
MESH = pl.DeviceIdType.MESH
CHAIN = 256


def softmax_step(s, v, state):
    m, l, acc = state
    mn = jnp.maximum(m, jnp.max(s, axis=1, keepdims=True))
    al = jnp.exp2((m - mn) * EXP2)
    p = jnp.exp2((s - mn) * EXP2)
    part = p[:, 0:HD]
    for t in range(1, s.shape[1] // HD):
        part = part + p[:, t * HD : (t + 1) * HD]
    acc = acc * al + jnp.dot(p.astype(jnp.bfloat16), v, preferred_element_type=jnp.float32)
    return mn, l * al + part, acc


def flash_chunk(qs, k, v, states, allowed):
    m_ref, l_ref, acc_ref = states

    def score(q):
        s = lax.dot_general(q, k, (((1,), (1,)), ((), ())), preferred_element_type=jnp.float32)
        return s if allowed is None else jnp.where(allowed, s, NEG)

    s = score(qs[0])
    for i in range(len(qs)):
        following = score(qs[i + 1]) if i + 1 < len(qs) else None
        here = pl.ds(i * CHAIN, CHAIN)
        m, l, acc = softmax_step(s, v, (m_ref[here, 0:1], l_ref[here, :], acc_ref[here, :]))
        m_ref[here, :] = jnp.broadcast_to(m, (CHAIN, HD))
        l_ref[here, :] = l
        acc_ref[here, :] = acc
        s = following


def kernel(
    pq_ref, pkv_ref, dest_ref, pool_ref, table_ref, len_ref, dq_ref, dn_ref,
    out_ref, arr_ref, dec_ref,
    kv, qin, obuf, pages, arr_send, pool, dq, dn, qd, dec_send, stat_send, dec_recv, stat_recv, fin, finb, finx,
    st_m, st_l, st_acc,
    local_sem, q_send, q_recv, kv_send, kv_recv, o_send, o_recv, a_send, a_recv,
    d_send, d_recv, s_send, s_recv, f_send, f_recv,
):
    c, g = lax.axis_index("ctx"), lax.axis_index("grp")
    x, y, z, co = c // 4, c % 4, g // 2, g % 2
    py = y // 2
    hy = (y % 2 + py) % 2
    k = x * 2 + hy
    ox = 1 - x
    yx = y + 1 - 2 * (y % 2)
    my = 3 - y
    myx = my + 1 - 2 * (my % 2)
    sib = z * 2 + 1 - co

    c_a, c_b, c_c = x * 4 + yx, ox * 4 + my, ox * 4 + myx
    q_peers = [(c_a, x * 2 + 1 - hy), (c_b, ox * 2 + hy), (c_c, ox * 2 + 1 - hy)]
    kv_peers = [(c_a, x * 2 + 1 - hy), (ox * 4 + y, ox * 2 + hy), (ox * 4 + yx, ox * 2 + 1 - hy)]

    def remote(src, dst, send, recv, cc, gg):
        return pltpu.make_async_remote_copy(
            src_ref=src, dst_ref=dst, send_sem=send, recv_sem=recv,
            device_id={"ctx": cc, "grp": gg}, device_id_type=MESH,
        )

    loads = [
        pltpu.make_async_copy(dq_ref, dq, local_sem.at[0]),
        pltpu.make_async_copy(pool_ref, pool, local_sem.at[3]),
        pltpu.make_async_copy(dn_ref, dn, local_sem.at[1]),
        pltpu.make_async_copy(pkv_ref, pages, local_sem.at[2]),
    ]
    own_q = pltpu.make_async_copy(pq_ref.at[:, pl.ds(pl.multiple_of(k * 1024, 1024), 1024)], qin.at[3], local_sem.at[4])
    own_kv = pltpu.make_async_copy(pkv_ref.at[:, pl.ds(pl.multiple_of(k * 256, 256), 256)], kv.at[x, y, g], local_sem.at[5])
    own_kv.start()
    for load in loads:
        load.start()
    own_q.start()

    barrier = pltpu.get_barrier_semaphore()
    partners = [((c + i) % 8, g) for i in range(1, 8)] + [(c, (g + i) % 8) for i in range(1, 8)]
    for cc, gg in partners:
        pl.semaphore_signal(barrier, inc=1, device_id={"ctx": cc, "grp": gg}, device_id_type=MESH)
    pl.semaphore_wait(barrier, len(partners))

    hops = (1, 3, 2)
    z_peers = [((z + d) % 4) * 2 + co for d in hops]
    z_from = [((z + 4 - d) % 4) * 2 + co for d in hops]
    s_from = [((z + 4 - d) % 4) * 2 + 1 - co for d in hops]
    mirror = x * 4 + my
    own_pieces = [c] + [cc for cc, kk in kv_peers]
    mirror_pieces = [mirror, x * 4 + myx, ox * 4 + my, ox * 4 + myx]
    hop_copies = []

    def piece(cc, gg):
        return kv.at[cc // 4, cc % 4, gg]

    def half(first, gg):
        return kv.at[:, pl.ds(2 * py if first else 2 - 2 * py, 2), gg]

    def send_on(src, at, cc, gg):
        hop_copies.append(remote(src, src, kv_send.at[at], kv_recv.at[at], cc, gg))
        hop_copies[-1].start()

    def arrived(src, at, cc, gg):
        remote(src, src, kv_send.at[at], kv_recv.at[at], cc, gg).wait_recv()

    def pass_on(p):
        here = piece(own_pieces[p], g)
        for i, gg in enumerate(z_peers):
            send_on(here, 7 + 3 * p + i, c, gg)
        send_on(here, 3 + p, mirror, g)
        send_on(here, 19 + p, c, sib)

    kv_first = []
    for i, (cc, kk) in enumerate(kv_peers):
        kv_first.append(
            remote(pkv_ref.at[:, pl.ds(pl.multiple_of(kk * 256, 256), 256)], piece(c, g), kv_send.at[i], kv_recv.at[i], cc, g)
        )
        kv_first[-1].start()
    own_kv.wait()
    pass_on(0)
    q_copies = []
    for i, (cc, kk) in enumerate(q_peers):
        q_copies.append(
            remote(pq_ref.at[:, pl.ds(pl.multiple_of(kk * 1024, 1024), 1024)], qin.at[i], q_send.at[i], q_recv.at[i], cc, g)
        )
        q_copies[-1].start()

    loads[0].wait()
    for t in range(4):
        for head in range(32):
            row = (head // 4) * 16 + t * 4 + head % 4
            qd[pl.ds(row, 32, stride=128), :] = dq[t, :, head * HD : (head + 1) * HD].astype(jnp.float32)

    for p in range(1, 4):
        arrived(piece(own_pieces[p], g), p - 1, own_pieces[p], g)
        pass_on(p)

    loads[1].wait()
    lane = lax.broadcasted_iota(jnp.int32, (128, 128), 1)
    stat_send[...] = jnp.zeros_like(stat_send)
    together = 4

    def requests(n, unused):
        numbers = [n * together + i for i in range(together)]
        kvs, scores = [], []
        for r in numbers:
            kvr = jnp.concatenate([pool[table_ref[j, r]] for j in range(4)], axis=0)
            q = qd[pl.ds(pl.multiple_of(r * 128, 128), 128), :].astype(jnp.bfloat16)
            s = jnp.concatenate(
                [
                    lax.dot_general(
                        q[h * 32 : (h + 1) * 32], kvr[:, h * 256 : h * 256 + 128],
                        (((1,), (1,)), ((), ())), preferred_element_type=jnp.float32,
                    )
                    for h in range(4)
                ],
                axis=0,
            )
            kvs.append(kvr)
            scores.append(s)
        oks = [lane + c * 128 < len_ref[r] for r in numbers]
        scores = [jnp.where(ok, s, NEG) for ok, s in zip(oks, scores)]
        tops = [jnp.max(s, axis=1, keepdims=True) for s in scores]
        expos = [jnp.where(ok, jnp.exp2((s - m) * EXP2), 0.0) for ok, s, m in zip(oks, scores, tops)]
        sums = [jnp.sum(p, axis=1, keepdims=True) for p in expos]
        stat = stat_send[...]
        for r, m, l in zip(numbers, tops, sums):
            stat = jnp.where(lane == r, m, jnp.where(lane == r + 32, l, stat))
        stat_send[...] = stat
        for r, kvr, p in zip(numbers, kvs, expos):
            pb = p.astype(jnp.bfloat16)
            for h in range(4):
                pv = jnp.dot(
                    pb[h * 32 : (h + 1) * 32], kvr[:, h * 256 + 128 : h * 256 + 256], preferred_element_type=jnp.float32
                ).astype(jnp.bfloat16)
                here = pl.ds(pl.multiple_of(r * 16, 16), 16)
                dec_send[2 * h, here, :] = pv[:16]
                dec_send[2 * h + 1, here, :] = pv[16:]
        return unused

    lax.fori_loop(0, 16 // together, requests, 0)
    lax.fori_loop(16 // together, 32 // together, requests, 0)

    loads[2].wait()
    h = c // 2
    q = jnp.concatenate(
        [qd[pl.ds(pl.multiple_of(r * 128 + c * 16, 16), 16), :] for r in range(32)], axis=0
    ).astype(jnp.bfloat16)
    knew = dn[:, :, pl.ds(pl.multiple_of(h * 256, 256), 128)].reshape(128, 128)
    vnew = dn[:, :, pl.ds(pl.multiple_of(h * 256 + 128, 128), 128)].reshape(128, 128)
    s = lax.dot_general(q, knew, (((1,), (1,)), ((), ())), preferred_element_type=jnp.float32)
    drow = lax.broadcasted_iota(jnp.int32, (512, 128), 0)
    dcol = lax.broadcasted_iota(jnp.int32, (512, 128), 1)
    ok = (dcol % 32 == drow // 16) & (dcol // 32 <= (drow % 16) // 4)
    s = jnp.where(ok, s, NEG)
    m_new = jnp.max(s, axis=1, keepdims=True)
    p = jnp.where(ok, jnp.exp2((s - m_new) * EXP2), 0.0)
    l_new = jnp.sum(p, axis=1, keepdims=True)
    fin[...] = jnp.dot(p.astype(jnp.bfloat16), vnew, preferred_element_type=jnp.float32)

    stat_recv[0] = jnp.sum(
        jnp.where(dcol == drow // 16, m_new, jnp.where(dcol == drow // 16 + 32, l_new, 0.0)).reshape(32, 16, 128), axis=0
    )
    st_m[...] = jnp.full_like(st_m, NEG)
    st_l[...] = jnp.zeros_like(st_l)
    st_acc[...] = jnp.zeros_like(st_acc)

    dec_copies = []
    for i in range(1, 8):
        cc = (c + i) % 8
        dec_copies.append(remote(dec_send.at[cc], dec_recv.at[i], d_send.at[i], d_recv.at[i], cc, g))
        dec_copies.append(
            remote(
                stat_send.at[pl.ds(pl.multiple_of(cc * 16, 16), 16)], stat_recv.at[i], s_send.at[i], s_recv.at[i], cc, g
            )
        )
    for p in range(4):
        for i, gg in enumerate(z_from):
            here = piece(own_pieces[p], gg)
            arrived(here, 7 + 3 * p + i, c, gg)
            send_on(here, 23 + 3 * p + i, c, sib)
    for p in range(4):
        arrived(piece(mirror_pieces[p], g), 3 + p, mirror, g)
    for i, gg in enumerate(z_peers):
        send_on(half(False, g), 35 + i, c, gg)
    send_on(half(False, g), 38, c, sib)

    for copy in dec_copies:
        copy.start()

    loads[3].wait()
    dests = [dest_ref[0, p] for p in range(4)]
    ranks = [sum([(dests[q] == dests[p]).astype(jnp.int32) for q in range(p)], jnp.int32(0)) for p in range(4)]
    marks = [dests[p] * 2 + ranks[p] for p in range(4)]

    def slot_page(i, unused):
        page = jnp.zeros((32, 1024), jnp.bfloat16)
        for p in range(4):
            hit = jnp.full((32, 1024), marks[p], jnp.int32) == i
            page = jnp.where(hit, pages[p * 32 : (p + 1) * 32, :], page)
        arr_send[i] = page
        return unused

    lax.fori_loop(0, 16, slot_page, 0)

    row = lax.broadcasted_iota(jnp.int32, (CHAIN, 1024), 0) % 128
    col = lax.broadcasted_iota(jnp.int32, (CHAIN, 1024), 1)
    allowed = col - row <= g * 128
    nchain = 1024 // CHAIN
    per = CHAIN // HD
    columns = pl.ds(pl.multiple_of(k * 1024, 1024), 1024)

    def queries_of(slot):
        return [
            jnp.concatenate([qin[slot, :, (i * per + j) * HD : (i * per + j + 1) * HD] for j in range(per)], axis=0)
            for i in range(nchain)
        ]

    def chunk(cc):
        both = kv[cc // 4, cc % 4].reshape(1024, 256)
        return both[:, :HD], both[:, HD:]

    def states_of(slot):
        return st_m.at[slot], st_l.at[slot], st_acc.at[slot]

    def over(slot, first, cs, diagonal):
        qs, states = queries_of(slot), states_of(slot)
        pair = 2 * py if first else 2 - 2 * py
        ids = [(j // 2) * 4 + pair + j % 2 for j in range(4)]
        count = sum([(one < cs).astype(jnp.int32) for one in ids], jnp.int32(0))

        def full(j, unused):
            flash_chunk(qs, *chunk((j // 2) * 4 + pair + j % 2), states, None)
            return unused

        lax.fori_loop(0, count, full, 0)

        @pl.when(diagonal)
        def _():
            flash_chunk(qs, *chunk(cs), states, allowed)

    def finish(slot):
        for i in range(nchain):
            here = pl.ds(i * CHAIN, CHAIN)
            o = (st_acc[slot, here, :] / jnp.sum(st_l[slot, here, :], axis=1, keepdims=True)).astype(jnp.bfloat16)
            for j in range(per):
                obuf[slot, :, (i * per + j) * HD : (i * per + j + 1) * HD] = o[j * HD : (j + 1) * HD]

    def pick(j):
        slot = jnp.where(j == 0, 0, jnp.where(j == 1, 3, jnp.where(j == 2, 2, 1)))
        return slot, jnp.where(j == 0, c_a, jnp.where(j == 1, c, jnp.where(j == 2, c_c, c_b)))

    def first_pass(j, unused):
        slot, cs = pick(j)

        @pl.when(j != 1)
        def _():
            remote(qin.at[slot], qin.at[slot], q_send.at[slot], q_recv.at[slot], cs, g).wait_recv()

        over(slot, True, cs, j == 0)
        return unused

    def second_pass(n, unused):
        j = (n + 2) % 4
        slot, cs = pick(j)
        over(slot, False, cs, j != 0)
        finish(slot)

        @pl.when(j != 1)
        def _():
            remote(obuf.at[slot], out_ref.at[:, columns], o_send.at[slot], o_recv.at[slot], cs, g).start()

        return unused

    own_q.wait()
    for p in range(4):
        arrived(piece(own_pieces[p], sib), 19 + p, c, sib)
        for i, gg in enumerate(s_from):
            arrived(piece(own_pieces[p], gg), 23 + 3 * p + i, c, sib)
    lax.fori_loop(0, 4, first_pass, 0)

    for i, gg in enumerate(z_from):
        arrived(half(False, gg), 35 + i, c, gg)
        send_on(half(False, gg), 39 + i, c, sib)
    arr_copies = []
    for i in range(1, 8):
        gg = (g + i) % 8
        arr_copies.append(
            remote(arr_send.at[pl.ds(2 * gg, 2)], arr_ref.at[pl.ds(2 * g, 2)], a_send.at[i], a_recv.at[i], c, gg)
        )
        arr_copies[-1].start()
    own_arr = pltpu.make_async_copy(arr_send.at[pl.ds(2 * g, 2)], arr_ref.at[pl.ds(2 * g, 2)], local_sem.at[6])
    own_arr.start()

    for i in range(1, 8):
        remote(dec_recv.at[i], dec_recv.at[i], d_send.at[i], d_recv.at[i], c, g).wait_recv()
        remote(stat_recv.at[i], stat_recv.at[i], s_send.at[i], s_recv.at[i], c, g).wait_recv()
    stats = [stat_recv[0], stat_send[pl.ds(pl.multiple_of(c * 16, 16), 16), :]] + [stat_recv[i] for i in range(1, 8)]
    tops = [stat[:, 0:32] for stat in stats]
    sums = [stat[:, 32:64] for stat in stats]
    top = tops[0]
    for other in tops[1:]:
        top = jnp.maximum(top, other)
    fixes = [jnp.exp2((other - top) * EXP2) for other in tops]
    total = fixes[0] * sums[0]
    for fix, part in zip(fixes[1:], sums[1:]):
        total = total + fix * part
    spread = dcol[:, 0:32] == drow[:, 0:32] // 16
    result = None
    for i, fix in enumerate(fixes):
        weight = jnp.sum(
            jnp.where(spread, jnp.concatenate([fix / total] * 32, axis=0), 0.0), axis=1, keepdims=True
        )
        part = fin[...] if i == 0 else (dec_send[c] if i == 1 else dec_recv[i - 1]).astype(jnp.float32)
        result = part * weight if result is None else result + part * weight
    fin[...] = result
    for t in range(4):
        for j in range(4):
            finb[t, :, j * HD : (j + 1) * HD] = fin[pl.ds(t * 4 + j, 32, stride=16), :].astype(jnp.bfloat16)
    dcols = pl.ds(pl.multiple_of(c * 512, 512), 512)
    own_dec = pltpu.make_async_copy(finb, dec_ref.at[:, :, dcols], local_sem.at[8])
    own_dec.start()
    across = ox * 4 + y
    f_copies = [remote(finb, finx, f_send.at[0], f_recv.at[0], across, g)]
    f_copies[0].start()
    for d in range(1, 4):
        f_copies.append(remote(finb, dec_ref.at[:, :, dcols], f_send.at[d], f_recv.at[d], x * 4 + (y + d) % 4, g))
        f_copies[-1].start()

    arrived(half(False, sib), 38, c, sib)
    for i, gg in enumerate(s_from):
        arrived(half(False, gg), 39 + i, c, sib)
    remote(finx, finx, f_send.at[0], f_recv.at[0], across, g).wait_recv()
    xcols = pl.ds(pl.multiple_of(across * 512, 512), 512)
    other_dec = pltpu.make_async_copy(finx, dec_ref.at[:, :, xcols], local_sem.at[9])
    other_dec.start()
    for d in range(1, 4):
        f_copies.append(remote(finx, dec_ref.at[:, :, xcols], f_send.at[3 + d], f_recv.at[3 + d], x * 4 + (y + d) % 4, g))
        f_copies[-1].start()
    lax.fori_loop(0, 4, second_pass, 0)
    own_out = pltpu.make_async_copy(obuf.at[3], out_ref.at[:, columns], local_sem.at[7])
    own_out.start()

    for i in range(1, 8):
        gg = (g + 8 - i) % 8
        here = arr_ref.at[pl.ds(2 * gg, 2)]
        remote(here, here, a_send.at[i], a_recv.at[i], c, gg).wait_recv()
        if i < 7:
            cc = (x if i < 4 else ox) * 4 + (y + 8 - (i if i < 4 else i - 3)) % 4
            here = dec_ref.at[:, :, pl.ds(pl.multiple_of(cc * 512, 512), 512)]
            remote(here, here, f_send.at[i], f_recv.at[i], cc, g).wait_recv()
    for i, (cc, kk) in enumerate(q_peers):
        here = out_ref.at[:, pl.ds(pl.multiple_of(kk * 1024, 1024), 1024)]
        remote(obuf.at[i], here, o_send.at[i], o_recv.at[i], cc, g).wait()
    for copy in kv_first + hop_copies + q_copies + dec_copies + arr_copies + f_copies:
        copy.wait_send()
    own_arr.wait()
    own_out.wait()
    own_dec.wait()
    other_dec.wait()


def hand_out(out_in, arr_in, dec_in, out_ref, arr_ref, dec_ref, out_buf, arr_buf, dec_buf, sem_in, sem_out):
    moves = []
    for src, buf, dst in ((out_in, out_buf, out_ref), (arr_in, arr_buf, arr_ref), (dec_in, dec_buf, dec_ref)):
        rows = src.shape[0] // 4
        for i in range(4):
            here = pl.ds(i * rows, rows)
            n = len(moves)
            moves.append(
                (
                    pltpu.make_async_copy(src.at[here], buf.at[here], sem_in.at[n]),
                    pltpu.make_async_copy(buf.at[here], dst.at[here], sem_out.at[n]),
                )
            )
    for load, store in moves:
        load.start()
    for load, store in moves:
        load.wait()
        store.start()
    for load, store in moves:
        store.wait()


def on_device(prefill_query, prefill_kv, page_dest, cache_pool, page_table, context_len, dec_query, dec_new):
    any_spec, smem = pl.BlockSpec(memory_space=pl.ANY), pl.BlockSpec(memory_space=pltpu.SMEM)
    bf16, f32 = jnp.bfloat16, jnp.float32
    dma = pltpu.SemaphoreType.DMA
    out, arrivals, dec = pl.pallas_call(
        kernel,
        out_shape=(
            jax.ShapeDtypeStruct((128, 4096), bf16),
            jax.ShapeDtypeStruct((16, 32, 1024), bf16),
            jax.ShapeDtypeStruct((4, 32, 4096), bf16),
        ),
        in_specs=[any_spec, any_spec, smem, any_spec, smem, smem, any_spec, any_spec],
        out_specs=(any_spec, any_spec, any_spec),
        scratch_shapes=[
            pltpu.VMEM((2, 4, 8, 128, 256), bf16),
            pltpu.VMEM((4, 128, 1024), bf16),
            pltpu.VMEM((4, 128, 1024), bf16),
            pltpu.VMEM((128, 1024), bf16),
            pltpu.VMEM((16, 32, 1024), bf16),
            pltpu.VMEM((128, 32, 1024), bf16),
            pltpu.VMEM((4, 32, 4096), bf16),
            pltpu.VMEM((4, 32, 1024), bf16),
            pltpu.VMEM((32 * 128, 128), f32),
            pltpu.VMEM((8, 512, 128), bf16),
            pltpu.VMEM((128, 128), f32),
            pltpu.VMEM((8, 512, 128), bf16),
            pltpu.VMEM((8, 16, 128), f32),
            pltpu.VMEM((512, 128), f32),
            pltpu.VMEM((4, 32, 512), bf16),
            pltpu.VMEM((4, 32, 512), bf16),
            pltpu.VMEM((4, 1024, 128), f32),
            pltpu.VMEM((4, 1024, 128), f32),
            pltpu.VMEM((4, 1024, 128), f32),
            dma((10,)),
            dma((3,)), dma((3,)), dma((42,)), dma((42,)), dma((3,)), dma((3,)),
            dma((8,)), dma((8,)), dma((8,)), dma((8,)), dma((8,)), dma((8,)), dma((8,)), dma((8,)),
        ],
        compiler_params=pltpu.CompilerParams(
            collective_id=0, has_side_effects=True, vmem_limit_bytes=58 * 2**20
        ),
        cost_estimate=pl.CostEstimate(flops=10**10, bytes_accessed=20 * 2**20, transcendentals=2 * 10**7),
        name="serving_step",
    )(
        prefill_query, prefill_kv, page_dest.T, cache_pool.reshape(128, 32, 1024), page_table.T, context_len,
        dec_query, dec_new,
    )
    out, arrivals, dec = pl.pallas_call(
        hand_out,
        out_shape=tuple(jax.ShapeDtypeStruct(a.shape, a.dtype) for a in (out, arrivals, dec)),
        in_specs=[pl.BlockSpec(memory_space=pltpu.HBM)] * 3,
        out_specs=(pl.BlockSpec(memory_space=pltpu.HBM),) * 3,
        scratch_shapes=[pltpu.VMEM(a.shape, a.dtype) for a in (out, arrivals, dec)] + [dma((12,)), dma((12,))],
        cost_estimate=pl.CostEstimate(flops=0, bytes_accessed=6 * 2**20, transcendentals=0),
        name="hand_out",
    )(out, arrivals, dec)
    return out, arrivals.reshape(1, 1, 16, 32, 1024), dec


def solution(mesh):
    placed = (
        P(("ctx", "grp"), "head"),
        P(("ctx", "grp"), "head"),
        P(("ctx", "grp"), None),
        P("ctx", "grp", None, None, "head"),
        P("grp", "ctx"),
        P("grp"),
        P(None, "grp", "head"),
        P(None, "grp", "head"),
    )
    return jax.shard_map(
        on_device,
        mesh=mesh,
        in_specs=placed,
        out_specs=(
            P(("ctx", "grp"), "head"),
            P("grp", "ctx", None, None, "head"),
            P(None, "grp", "head"),
        ),
        check_vma=False,
    )
```

```python
import jax
import jax.numpy as jnp
from jax import lax
from jax.experimental import pallas as pl
from jax.experimental.pallas import tpu as pltpu
from jax.sharding import PartitionSpec as P

HD = 128
NEG = -1e30
SCALE = HD**-0.5
EXP2 = SCALE * 1.4426950408889634
MESH = pl.DeviceIdType.MESH
CHAIN = 256


def softmax_step(s, v, state):
    m, l, acc = state
    mn = jnp.maximum(m, jnp.max(s, axis=1, keepdims=True))
    al = jnp.exp2((m - mn) * EXP2)
    p = jnp.exp2((s - mn) * EXP2)
    part = p[:, 0:HD]
    for t in range(1, s.shape[1] // HD):
        part = part + p[:, t * HD : (t + 1) * HD]
    acc = acc * al + jnp.dot(p.astype(jnp.bfloat16), v, preferred_element_type=jnp.float32)
    return mn, l * al + part, acc


def flash_chunk(qs, k, v, states, allowed):
    m_ref, l_ref, acc_ref = states

    def score(q):
        s = lax.dot_general(q, k, (((1,), (1,)), ((), ())), preferred_element_type=jnp.float32)
        return s if allowed is None else jnp.where(allowed, s, NEG)

    s = score(qs[0])
    for i in range(len(qs)):
        following = score(qs[i + 1]) if i + 1 < len(qs) else None
        here = pl.ds(i * CHAIN, CHAIN)
        m, l, acc = softmax_step(s, v, (m_ref[here, 0:1], l_ref[here, :], acc_ref[here, :]))
        m_ref[here, :] = jnp.broadcast_to(m, (CHAIN, HD))
        l_ref[here, :] = l
        acc_ref[here, :] = acc
        s = following


def kernel(
    pq_ref, pkv_ref, dest_ref, pool_ref, table_ref, len_ref, dq_ref, dn_ref,
    out_ref, arr_ref, dec_ref,
    kv, qin, obuf, pages, arr_send, pool, dq, dn, qd, dec_send, stat_send, dec_recv, stat_recv, fin, finb, finx,
    st_m, st_l, st_acc,
    local_sem, q_send, q_recv, kv_send, kv_recv, o_send, o_recv, a_send, a_recv,
    d_send, d_recv, s_send, s_recv, f_send, f_recv,
):
    c, g = lax.axis_index("ctx"), lax.axis_index("grp")
    x, y, z, co = c // 4, c % 4, g // 2, g % 2
    py = y // 2
    hy = (y % 2 + py) % 2
    k = x * 2 + hy
    ox = 1 - x
    yx = y + 1 - 2 * (y % 2)
    my = 3 - y
    myx = my + 1 - 2 * (my % 2)
    sib = z * 2 + 1 - co

    c_a, c_b, c_c = x * 4 + yx, ox * 4 + my, ox * 4 + myx
    q_peers = [(c_a, x * 2 + 1 - hy), (c_b, ox * 2 + hy), (c_c, ox * 2 + 1 - hy)]
    kv_peers = [(c_a, x * 2 + 1 - hy), (ox * 4 + y, ox * 2 + hy), (ox * 4 + yx, ox * 2 + 1 - hy)]

    def remote(src, dst, send, recv, cc, gg):
        return pltpu.make_async_remote_copy(
            src_ref=src, dst_ref=dst, send_sem=send, recv_sem=recv,
            device_id={"ctx": cc, "grp": gg}, device_id_type=MESH,
        )

    loads = [
        pltpu.make_async_copy(dq_ref, dq, local_sem.at[0]),
        pltpu.make_async_copy(pool_ref, pool, local_sem.at[3]),
        pltpu.make_async_copy(dn_ref, dn, local_sem.at[1]),
        pltpu.make_async_copy(pkv_ref, pages, local_sem.at[2]),
    ]
    own_q = pltpu.make_async_copy(pq_ref.at[:, pl.ds(pl.multiple_of(k * 1024, 1024), 1024)], qin.at[3], local_sem.at[4])
    own_kv = pltpu.make_async_copy(pkv_ref.at[:, pl.ds(pl.multiple_of(k * 256, 256), 256)], kv.at[x, y, g], local_sem.at[5])
    own_kv.start()
    for load in loads:
        load.start()
    own_q.start()

    barrier = pltpu.get_barrier_semaphore()
    partners = [((c + i) % 8, g) for i in range(1, 8)] + [(c, (g + i) % 8) for i in range(1, 8)]
    for cc, gg in partners:
        pl.semaphore_signal(barrier, inc=1, device_id={"ctx": cc, "grp": gg}, device_id_type=MESH)
    pl.semaphore_wait(barrier, len(partners))

    hops = (1, 3, 2)
    z_peers = [((z + d) % 4) * 2 + co for d in hops]
    z_from = [((z + 4 - d) % 4) * 2 + co for d in hops]
    s_from = [((z + 4 - d) % 4) * 2 + 1 - co for d in hops]
    mirror = x * 4 + my
    own_pieces = [c] + [cc for cc, kk in kv_peers]
    mirror_pieces = [mirror, x * 4 + myx, ox * 4 + my, ox * 4 + myx]
    hop_copies = []

    def piece(cc, gg):
        return kv.at[cc // 4, cc % 4, gg]

    def half(first, gg):
        return kv.at[:, pl.ds(2 * py if first else 2 - 2 * py, 2), gg]

    def send_on(src, at, cc, gg):
        hop_copies.append(remote(src, src, kv_send.at[at], kv_recv.at[at], cc, gg))
        hop_copies[-1].start()

    def arrived(src, at, cc, gg):
        remote(src, src, kv_send.at[at], kv_recv.at[at], cc, gg).wait_recv()

    def pass_on(p):
        here = piece(own_pieces[p], g)
        for i, gg in enumerate(z_peers):
            send_on(here, 7 + 3 * p + i, c, gg)
        send_on(here, 3 + p, mirror, g)
        send_on(here, 19 + p, c, sib)

    kv_first = []
    for i, (cc, kk) in enumerate(kv_peers):
        kv_first.append(
            remote(pkv_ref.at[:, pl.ds(pl.multiple_of(kk * 256, 256), 256)], piece(c, g), kv_send.at[i], kv_recv.at[i], cc, g)
        )
        kv_first[-1].start()
    own_kv.wait()
    pass_on(0)
    q_copies = []
    for i, (cc, kk) in enumerate(q_peers):
        q_copies.append(
            remote(pq_ref.at[:, pl.ds(pl.multiple_of(kk * 1024, 1024), 1024)], qin.at[i], q_send.at[i], q_recv.at[i], cc, g)
        )
        q_copies[-1].start()

    loads[0].wait()
    for t in range(4):
        for head in range(32):
            row = (head // 4) * 16 + t * 4 + head % 4
            qd[pl.ds(row, 32, stride=128), :] = dq[t, :, head * HD : (head + 1) * HD].astype(jnp.float32)

    for p in range(1, 4):
        arrived(piece(own_pieces[p], g), p - 1, own_pieces[p], g)
        pass_on(p)

    loads[1].wait()
    lane = lax.broadcasted_iota(jnp.int32, (128, 128), 1)
    stat_send[...] = jnp.zeros_like(stat_send)
    together = 8

    def requests(n, unused):
        numbers = [n * together + i for i in range(together)]
        kvs, scores = [], []
        for r in numbers:
            kvr = jnp.concatenate([pool[table_ref[j, r]] for j in range(4)], axis=0)
            q = qd[pl.ds(pl.multiple_of(r * 128, 128), 128), :].astype(jnp.bfloat16)
            s = jnp.concatenate(
                [
                    lax.dot_general(
                        q[h * 32 : (h + 1) * 32], kvr[:, h * 256 : h * 256 + 128],
                        (((1,), (1,)), ((), ())), preferred_element_type=jnp.float32,
                    )
                    for h in range(4)
                ],
                axis=0,
            )
            kvs.append(kvr)
            scores.append(s)
        oks = [lane + c * 128 < len_ref[r] for r in numbers]
        scores = [jnp.where(ok, s, NEG) for ok, s in zip(oks, scores)]
        tops = [jnp.max(s, axis=1, keepdims=True) for s in scores]
        expos = [jnp.where(ok, jnp.exp2((s - m) * EXP2), 0.0) for ok, s, m in zip(oks, scores, tops)]
        sums = [jnp.sum(p, axis=1, keepdims=True) for p in expos]
        stat = stat_send[...]
        for r, m, l in zip(numbers, tops, sums):
            stat = jnp.where(lane == r, m, jnp.where(lane == r + 32, l, stat))
        stat_send[...] = stat
        for r, kvr, p in zip(numbers, kvs, expos):
            pb = p.astype(jnp.bfloat16)
            for h in range(4):
                pv = jnp.dot(
                    pb[h * 32 : (h + 1) * 32], kvr[:, h * 256 + 128 : h * 256 + 256], preferred_element_type=jnp.float32
                ).astype(jnp.bfloat16)
                here = pl.ds(pl.multiple_of(r * 16, 16), 16)
                dec_send[2 * h, here, :] = pv[:16]
                dec_send[2 * h + 1, here, :] = pv[16:]
        return unused

    lax.fori_loop(0, 16 // together, requests, 0)
    lax.fori_loop(16 // together, 32 // together, requests, 0)

    loads[2].wait()
    h = c // 2
    q = jnp.concatenate(
        [qd[pl.ds(pl.multiple_of(r * 128 + c * 16, 16), 16), :] for r in range(32)], axis=0
    ).astype(jnp.bfloat16)
    knew = dn[:, :, pl.ds(pl.multiple_of(h * 256, 256), 128)].reshape(128, 128)
    vnew = dn[:, :, pl.ds(pl.multiple_of(h * 256 + 128, 128), 128)].reshape(128, 128)
    s = lax.dot_general(q, knew, (((1,), (1,)), ((), ())), preferred_element_type=jnp.float32)
    drow = lax.broadcasted_iota(jnp.int32, (512, 128), 0)
    dcol = lax.broadcasted_iota(jnp.int32, (512, 128), 1)
    ok = (dcol % 32 == drow // 16) & (dcol // 32 <= (drow % 16) // 4)
    s = jnp.where(ok, s, NEG)
    m_new = jnp.max(s, axis=1, keepdims=True)
    p = jnp.where(ok, jnp.exp2((s - m_new) * EXP2), 0.0)
    l_new = jnp.sum(p, axis=1, keepdims=True)
    fin[...] = jnp.dot(p.astype(jnp.bfloat16), vnew, preferred_element_type=jnp.float32)

    stat_recv[0] = jnp.sum(
        jnp.where(dcol == drow // 16, m_new, jnp.where(dcol == drow // 16 + 32, l_new, 0.0)).reshape(32, 16, 128), axis=0
    )
    st_m[...] = jnp.full_like(st_m, NEG)
    st_l[...] = jnp.zeros_like(st_l)
    st_acc[...] = jnp.zeros_like(st_acc)

    dec_copies = []
    for i in (4, 3, 5, 1, 7, 2, 6):
        cc = (c + i) % 8
        dec_copies.append(remote(dec_send.at[cc], dec_recv.at[i], d_send.at[i], d_recv.at[i], cc, g))
        dec_copies.append(
            remote(
                stat_send.at[pl.ds(pl.multiple_of(cc * 16, 16), 16)], stat_recv.at[i], s_send.at[i], s_recv.at[i], cc, g
            )
        )
    for p in range(4):
        for i, gg in enumerate(z_from):
            here = piece(own_pieces[p], gg)
            arrived(here, 7 + 3 * p + i, c, gg)
            send_on(here, 23 + 3 * p + i, c, sib)
    for p in range(4):
        arrived(piece(mirror_pieces[p], g), 3 + p, mirror, g)
    for i, gg in enumerate(z_peers):
        send_on(half(False, g), 35 + i, c, gg)
    send_on(half(False, g), 38, c, sib)

    for copy in dec_copies:
        copy.start()

    loads[3].wait()
    dests = [dest_ref[0, p] for p in range(4)]
    ranks = [sum([(dests[q] == dests[p]).astype(jnp.int32) for q in range(p)], jnp.int32(0)) for p in range(4)]
    marks = [dests[p] * 2 + ranks[p] for p in range(4)]

    def slot_page(i, unused):
        page = jnp.zeros((32, 1024), jnp.bfloat16)
        for p in range(4):
            hit = jnp.full((32, 1024), marks[p], jnp.int32) == i
            page = jnp.where(hit, pages[p * 32 : (p + 1) * 32, :], page)
        arr_send[i] = page
        return unused

    lax.fori_loop(0, 16, slot_page, 0)

    row = lax.broadcasted_iota(jnp.int32, (CHAIN, 1024), 0) % 128
    col = lax.broadcasted_iota(jnp.int32, (CHAIN, 1024), 1)
    allowed = col - row <= g * 128
    nchain = 1024 // CHAIN
    per = CHAIN // HD
    columns = pl.ds(pl.multiple_of(k * 1024, 1024), 1024)

    def queries_of(slot):
        return [
            jnp.concatenate([qin[slot, :, (i * per + j) * HD : (i * per + j + 1) * HD] for j in range(per)], axis=0)
            for i in range(nchain)
        ]

    def chunk(cc):
        both = kv[cc // 4, cc % 4].reshape(1024, 256)
        return both[:, :HD], both[:, HD:]

    def states_of(slot):
        return st_m.at[slot], st_l.at[slot], st_acc.at[slot]

    def over(slot, first, cs, diagonal):
        qs, states = queries_of(slot), states_of(slot)
        pair = 2 * py if first else 2 - 2 * py
        ids = [(j // 2) * 4 + pair + j % 2 for j in range(4)]
        count = sum([(one < cs).astype(jnp.int32) for one in ids], jnp.int32(0))

        def full(j, unused):
            flash_chunk(qs, *chunk((j // 2) * 4 + pair + j % 2), states, None)
            return unused

        lax.fori_loop(0, count, full, 0)

        @pl.when(diagonal)
        def _():
            flash_chunk(qs, *chunk(cs), states, allowed)

    def finish(slot):
        for i in range(nchain):
            here = pl.ds(i * CHAIN, CHAIN)
            o = (st_acc[slot, here, :] / jnp.sum(st_l[slot, here, :], axis=1, keepdims=True)).astype(jnp.bfloat16)
            for j in range(per):
                obuf[slot, :, (i * per + j) * HD : (i * per + j + 1) * HD] = o[j * HD : (j + 1) * HD]

    def pick(j):
        slot = jnp.where(j == 0, 0, jnp.where(j == 1, 3, jnp.where(j == 2, 2, 1)))
        return slot, jnp.where(j == 0, c_a, jnp.where(j == 1, c, jnp.where(j == 2, c_c, c_b)))

    def first_pass(j, unused):
        slot, cs = pick(j)

        @pl.when(j != 1)
        def _():
            remote(qin.at[slot], qin.at[slot], q_send.at[slot], q_recv.at[slot], cs, g).wait_recv()

        over(slot, True, cs, j == 0)
        return unused

    def second_pass(n, unused):
        j = (n + 2) % 4
        slot, cs = pick(j)
        over(slot, False, cs, j != 0)
        finish(slot)

        @pl.when(j != 1)
        def _():
            remote(obuf.at[slot], out_ref.at[:, columns], o_send.at[slot], o_recv.at[slot], cs, g).start()

        return unused

    own_q.wait()
    for p in range(4):
        arrived(piece(own_pieces[p], sib), 19 + p, c, sib)
        for i, gg in enumerate(s_from):
            arrived(piece(own_pieces[p], gg), 23 + 3 * p + i, c, sib)
    lax.fori_loop(0, 4, first_pass, 0)

    for i, gg in enumerate(z_from):
        arrived(half(False, gg), 35 + i, c, gg)
        send_on(half(False, gg), 39 + i, c, sib)
    arr_copies = []
    for i in range(1, 8):
        gg = (g + i) % 8
        arr_copies.append(
            remote(arr_send.at[pl.ds(2 * gg, 2)], arr_ref.at[pl.ds(2 * g, 2)], a_send.at[i], a_recv.at[i], c, gg)
        )
        arr_copies[-1].start()
    own_arr = pltpu.make_async_copy(arr_send.at[pl.ds(2 * g, 2)], arr_ref.at[pl.ds(2 * g, 2)], local_sem.at[6])
    own_arr.start()

    for i in range(1, 8):
        remote(dec_recv.at[i], dec_recv.at[i], d_send.at[i], d_recv.at[i], c, g).wait_recv()
        remote(stat_recv.at[i], stat_recv.at[i], s_send.at[i], s_recv.at[i], c, g).wait_recv()
    stats = [stat_recv[0], stat_send[pl.ds(pl.multiple_of(c * 16, 16), 16), :]] + [stat_recv[i] for i in range(1, 8)]
    tops = [stat[:, 0:32] for stat in stats]
    sums = [stat[:, 32:64] for stat in stats]
    top = tops[0]
    for other in tops[1:]:
        top = jnp.maximum(top, other)
    fixes = [jnp.exp2((other - top) * EXP2) for other in tops]
    total = fixes[0] * sums[0]
    for fix, part in zip(fixes[1:], sums[1:]):
        total = total + fix * part
    spread = dcol[:, 0:32] == drow[:, 0:32] // 16
    result = None
    for i, fix in enumerate(fixes):
        weight = jnp.sum(
            jnp.where(spread, jnp.concatenate([fix / total] * 32, axis=0), 0.0), axis=1, keepdims=True
        )
        part = fin[...] if i == 0 else (dec_send[c] if i == 1 else dec_recv[i - 1]).astype(jnp.float32)
        result = part * weight if result is None else result + part * weight
    fin[...] = result
    for t in range(4):
        for j in range(4):
            finb[t, :, j * HD : (j + 1) * HD] = fin[pl.ds(t * 4 + j, 32, stride=16), :].astype(jnp.bfloat16)
    dcols = pl.ds(pl.multiple_of(c * 512, 512), 512)
    own_dec = pltpu.make_async_copy(finb, dec_ref.at[:, :, dcols], local_sem.at[8])
    own_dec.start()
    across = ox * 4 + y
    f_copies = [remote(finb, finx, f_send.at[0], f_recv.at[0], across, g)]
    f_copies[0].start()
    for d in range(1, 4):
        f_copies.append(remote(finb, dec_ref.at[:, :, dcols], f_send.at[d], f_recv.at[d], x * 4 + (y + d) % 4, g))
        f_copies[-1].start()

    arrived(half(False, sib), 38, c, sib)
    for i, gg in enumerate(s_from):
        arrived(half(False, gg), 39 + i, c, sib)
    remote(finx, finx, f_send.at[0], f_recv.at[0], across, g).wait_recv()
    xcols = pl.ds(pl.multiple_of(across * 512, 512), 512)
    other_dec = pltpu.make_async_copy(finx, dec_ref.at[:, :, xcols], local_sem.at[9])
    other_dec.start()
    for d in range(1, 4):
        f_copies.append(remote(finx, dec_ref.at[:, :, xcols], f_send.at[3 + d], f_recv.at[3 + d], x * 4 + (y + d) % 4, g))
        f_copies[-1].start()
    lax.fori_loop(0, 4, second_pass, 0)
    own_out = pltpu.make_async_copy(obuf.at[3], out_ref.at[:, columns], local_sem.at[7])
    own_out.start()

    for i in range(1, 8):
        gg = (g + 8 - i) % 8
        here = arr_ref.at[pl.ds(2 * gg, 2)]
        remote(here, here, a_send.at[i], a_recv.at[i], c, gg).wait_recv()
        if i < 7:
            cc = (x if i < 4 else ox) * 4 + (y + 8 - (i if i < 4 else i - 3)) % 4
            here = dec_ref.at[:, :, pl.ds(pl.multiple_of(cc * 512, 512), 512)]
            remote(here, here, f_send.at[i], f_recv.at[i], cc, g).wait_recv()
    for i, (cc, kk) in enumerate(q_peers):
        here = out_ref.at[:, pl.ds(pl.multiple_of(kk * 1024, 1024), 1024)]
        remote(obuf.at[i], here, o_send.at[i], o_recv.at[i], cc, g).wait()
    for copy in kv_first + hop_copies + q_copies + dec_copies + arr_copies + f_copies:
        copy.wait_send()
    own_arr.wait()
    own_out.wait()
    own_dec.wait()
    other_dec.wait()


def hand_out(out_in, arr_in, dec_in, out_ref, arr_ref, dec_ref, out_buf, arr_buf, dec_buf, sem_in, sem_out):
    moves = []
    for src, buf, dst in ((out_in, out_buf, out_ref), (arr_in, arr_buf, arr_ref), (dec_in, dec_buf, dec_ref)):
        rows = src.shape[0] // 4
        for i in range(4):
            here = pl.ds(i * rows, rows)
            n = len(moves)
            moves.append(
                (
                    pltpu.make_async_copy(src.at[here], buf.at[here], sem_in.at[n]),
                    pltpu.make_async_copy(buf.at[here], dst.at[here], sem_out.at[n]),
                )
            )
    for load, store in moves:
        load.start()
    for load, store in moves:
        load.wait()
        store.start()
    for load, store in moves:
        store.wait()


def on_device(prefill_query, prefill_kv, page_dest, cache_pool, page_table, context_len, dec_query, dec_new):
    any_spec, smem = pl.BlockSpec(memory_space=pl.ANY), pl.BlockSpec(memory_space=pltpu.SMEM)
    bf16, f32 = jnp.bfloat16, jnp.float32
    dma = pltpu.SemaphoreType.DMA
    out, arrivals, dec = pl.pallas_call(
        kernel,
        out_shape=(
            jax.ShapeDtypeStruct((128, 4096), bf16),
            jax.ShapeDtypeStruct((16, 32, 1024), bf16),
            jax.ShapeDtypeStruct((4, 32, 4096), bf16),
        ),
        in_specs=[any_spec, any_spec, smem, any_spec, smem, smem, any_spec, any_spec],
        out_specs=(any_spec, any_spec, any_spec),
        scratch_shapes=[
            pltpu.VMEM((2, 4, 8, 128, 256), bf16),
            pltpu.VMEM((4, 128, 1024), bf16),
            pltpu.VMEM((4, 128, 1024), bf16),
            pltpu.VMEM((128, 1024), bf16),
            pltpu.VMEM((16, 32, 1024), bf16),
            pltpu.VMEM((128, 32, 1024), bf16),
            pltpu.VMEM((4, 32, 4096), bf16),
            pltpu.VMEM((4, 32, 1024), bf16),
            pltpu.VMEM((32 * 128, 128), f32),
            pltpu.VMEM((8, 512, 128), bf16),
            pltpu.VMEM((128, 128), f32),
            pltpu.VMEM((8, 512, 128), bf16),
            pltpu.VMEM((8, 16, 128), f32),
            pltpu.VMEM((512, 128), f32),
            pltpu.VMEM((4, 32, 512), bf16),
            pltpu.VMEM((4, 32, 512), bf16),
            pltpu.VMEM((4, 1024, 128), f32),
            pltpu.VMEM((4, 1024, 128), f32),
            pltpu.VMEM((4, 1024, 128), f32),
            dma((10,)),
            dma((3,)), dma((3,)), dma((42,)), dma((42,)), dma((3,)), dma((3,)),
            dma((8,)), dma((8,)), dma((8,)), dma((8,)), dma((8,)), dma((8,)), dma((8,)), dma((8,)),
        ],
        compiler_params=pltpu.CompilerParams(
            collective_id=0, has_side_effects=True, vmem_limit_bytes=58 * 2**20
        ),
        cost_estimate=pl.CostEstimate(flops=10**10, bytes_accessed=20 * 2**20, transcendentals=2 * 10**7),
        name="serving_step",
    )(
        prefill_query, prefill_kv, page_dest.T, cache_pool.reshape(128, 32, 1024), page_table.T, context_len,
        dec_query, dec_new,
    )
    out, arrivals, dec = pl.pallas_call(
        hand_out,
        out_shape=tuple(jax.ShapeDtypeStruct(a.shape, a.dtype) for a in (out, arrivals, dec)),
        in_specs=[pl.BlockSpec(memory_space=pltpu.HBM)] * 3,
        out_specs=(pl.BlockSpec(memory_space=pltpu.HBM),) * 3,
        scratch_shapes=[pltpu.VMEM(a.shape, a.dtype) for a in (out, arrivals, dec)] + [dma((12,)), dma((12,))],
        cost_estimate=pl.CostEstimate(flops=0, bytes_accessed=6 * 2**20, transcendentals=0),
        name="hand_out",
    )(out, arrivals, dec)
    return out, arrivals.reshape(1, 1, 16, 32, 1024), dec


def solution(mesh):
    placed = (
        P(("ctx", "grp"), "head"),
        P(("ctx", "grp"), "head"),
        P(("ctx", "grp"), None),
        P("ctx", "grp", None, None, "head"),
        P("grp", "ctx"),
        P("grp"),
        P(None, "grp", "head"),
        P(None, "grp", "head"),
    )
    return jax.shard_map(
        on_device,
        mesh=mesh,
        in_specs=placed,
        out_specs=(
            P(("ctx", "grp"), "head"),
            P("grp", "ctx", None, None, "head"),
            P(None, "grp", "head"),
        ),
        check_vma=False,
    )
```
